256 devices in a mesh: wide: 32 (over y, z), narrow: 8 (over x, core).
Axes of the slice: x: 4, y: 4, z: 8, core: 2. Of those that a mesh axis runs over, the one named last changes fastest.
Arguments:
- section_start: float32 [64, 32, 5, 27, 128], P('wide', 'narrow'), may hold values from -2 to 8, as said below
- section_state: float32 [64, 32, 5, 27, 128], P('wide', 'narrow'), may hold values from -2 to 8, as said below
- cut_code: int32 [64, 128], P('wide'), may hold values from 0 to 3
- cut_rule: int32 [64, 128], P('wide'), may hold values from 0 to 63
- rule_fractions: float32 [64, 27], replicated, may hold values from 0.05 to 0.5
Outputs:
- advanced: float32 [64, 32, 5, 27, 128], P('wide', 'narrow')
The draws below stay inside these ranges and needn't reach their ends.
Inputs may be any that keep to these rules, and one draw needn't show every extreme that they name: `section_start`: each node's density lies in [0.5, 2], its velocity components in [-1, 1] and its pressure in [0.5, 2]. `section_state`: each node's density lies in [0.5, 2], its velocity components in [-1, 1] and its pressure in [0.5, 2].
All inputs are finite; a program needn't handle non-finite values.
Results may differ from the reference program's by a relative error of at most 0.0003.
Values sent between devices are 32-bit elements; how exact they have to be, the bound alone decides.
No kernel may reach another device: no remote copies, remote signals or barrier semaphores. Data moves between devices by JAX's collectives and lax.ppermute only.
A program may use at most 64 MiB of HBM per device.

```python
import math
import jax
import jax.numpy as jnp
import numpy as np
from jax import lax

SPANWISE = 128
ELEMENT_NODES = 27
QUAD_RULES = 64
GRID_X = 64
GRID_Y = 32


ADIABATIC = 1.4


def conserved_fields(density, velocity, pressure):
    momentum = density[:, :, None] * velocity
    kinetic = velocity[:, :, 0] * velocity[:, :, 0] + velocity[:, :, 1] * velocity[:, :, 1] + velocity[:, :, 2] * velocity[:, :, 2]
    energy = pressure / (ADIABATIC - 1.0) + 0.5 * density * kinetic
    return jnp.concatenate([density[:, :, None], momentum, energy[:, :, None]], axis=2)


def draw_section_start(key, part):
    key = jax.random.fold_in(key, 13)
    subkeys = jax.random.split(key, 3)
    node_shape = (GRID_X, GRID_Y, ELEMENT_NODES, SPANWISE)
    velocity_shape = (GRID_X, GRID_Y, 3, ELEMENT_NODES, SPANWISE)
    density = jnp.exp(jax.random.uniform(subkeys[0], node_shape, jnp.float32, -0.69, 0.69))
    velocity = 0.5 * jnp.clip(jax.random.normal(subkeys[1], velocity_shape, jnp.float32), -2.0, 2.0)
    pressure = jnp.exp(jax.random.uniform(subkeys[2], node_shape, jnp.float32, -0.69, 0.69))
    return conserved_fields(density, velocity, pressure)


def draw_section_state(key, part):
    key = jax.random.fold_in(key, 7)
    subkeys = jax.random.split(key, 3)
    node_shape = (GRID_X, GRID_Y, ELEMENT_NODES, SPANWISE)
    velocity_shape = (GRID_X, GRID_Y, 3, ELEMENT_NODES, SPANWISE)
    density = jnp.exp(jax.random.uniform(subkeys[0], node_shape, jnp.float32, -0.69, 0.69))
    velocity = 0.5 * jnp.clip(jax.random.normal(subkeys[1], velocity_shape, jnp.float32), -2.0, 2.0)
    pressure = jnp.exp(jax.random.uniform(subkeys[2], node_shape, jnp.float32, -0.69, 0.69))
    return conserved_fields(density, velocity, pressure)


def touch_ends(drawn, key, least, high):
    shape = drawn.shape
    index_at = [jax.random.randint(jax.random.fold_in(key, axis), (), 0, shape[axis]) for axis in range(len(shape))]
    drawn = drawn.at[tuple(index_at)].set(least)
    longest = shape.index(max(shape))
    index_at[longest] = (index_at[longest] + 1) % shape[longest]
    return drawn.at[tuple(index_at)].set(high)


def setup_inputs(seed: int = 0) -> dict:
    keys = jax.random.split(jax.random.key(seed), 6)
    section_start = draw_section_start(jax.random.fold_in(keys[5], 71), 0)
    section_state = draw_section_state(jax.random.fold_in(keys[5], 71), 0)
    cut_code = touch_ends(jax.random.randint(keys[2], (GRID_X, SPANWISE), 0, 4), jax.random.fold_in(keys[2], 1), 0, 3).astype(jnp.int32)
    cut_rule = touch_ends(jax.random.randint(keys[3], (GRID_X, SPANWISE), 0, QUAD_RULES), jax.random.fold_in(keys[3], 1), 0, QUAD_RULES - 1).astype(jnp.int32)
    rule_fractions = jnp.clip(jnp.exp(jax.random.uniform(keys[4], (QUAD_RULES, ELEMENT_NODES), jnp.float32, math.log(0.05), math.log(0.5))), 0.05, 0.5)
    return dict(section_start=section_start, section_state=section_state, cut_code=cut_code, cut_rule=cut_rule, rule_fractions=rule_fractions)


HEAT_RATIO = 1.4
VISCOSITY = 0.1
TIME_STEP = 0.03
LIFT_FACTOR = 3.0

def node_layer(values, axis_node, index):
    return lax.index_in_dim(values, index, axis_node, keepdims=True)

def element_range(values, axis_elem, start, limit):
    return lax.slice_in_dim(values, start, limit, axis=axis_elem)

def derivative(values, axis_node):
    lowest = node_layer(values, axis_node, 0)
    middle = node_layer(values, axis_node, 1)
    highest = node_layer(values, axis_node, 2)
    return jnp.concatenate([-1.5 * lowest + 2.0 * middle - 0.5 * highest, 0.5 * (highest - lowest), 0.5 * lowest - 2.0 * middle + 1.5 * highest], axis=axis_node)

def physical_flux(fields, direction):
    density = fields[:, :, 0]
    momenta = [fields[:, :, 1], fields[:, :, 2], fields[:, :, 3]]
    energy = fields[:, :, 4]
    velocity = momenta[direction] / density
    kinetic = momenta[0] * momenta[0] + momenta[1] * momenta[1] + momenta[2] * momenta[2]
    pressure = (HEAT_RATIO - 1.0) * (energy - 0.5 * kinetic / density)
    components = [momenta[direction], momenta[0] * velocity, momenta[1] * velocity, momenta[2] * velocity, (energy + pressure) * velocity]
    components[1 + direction] = components[1 + direction] + pressure
    wave_speed = jnp.abs(velocity) + jnp.sqrt(HEAT_RATIO * pressure / density)
    return (jnp.stack(components, axis=2), wave_speed)

def riemann_flux(minus_side, plus_side, direction):
    flux_minus, speed_minus = physical_flux(minus_side, direction)
    flux_plus, speed_plus = physical_flux(plus_side, direction)
    largest = jnp.expand_dims(jnp.maximum(speed_minus, speed_plus), 2)
    return 0.5 * (flux_minus + flux_plus) - 0.5 * largest * (plus_side - minus_side)

def face_states(values, axis_elem, axis_node, lower_trace, upper_trace):
    minus_side = jnp.concatenate([lower_trace, node_layer(values, axis_node, 2)], axis=axis_elem)
    plus_side = jnp.concatenate([node_layer(values, axis_node, 0), upper_trace], axis=axis_elem)
    return (minus_side, plus_side)

def gradient_of(fields, minus_side, plus_side, axis_elem, axis_node):
    length = fields.shape[axis_elem]
    face_mean = 0.5 * (minus_side + plus_side)
    lower_face = element_range(face_mean, axis_elem, 0, length)
    upper_face = element_range(face_mean, axis_elem, 1, length + 1)
    slopes = derivative(fields, axis_node)
    lowest = node_layer(slopes, axis_node, 0) - LIFT_FACTOR * (lower_face - node_layer(fields, axis_node, 0))
    middle = node_layer(slopes, axis_node, 1)
    highest = node_layer(slopes, axis_node, 2) + LIFT_FACTOR * (upper_face - node_layer(fields, axis_node, 2))
    return jnp.concatenate([lowest, middle, highest], axis=axis_node)

def divergence(fields, slopes, minus_side, plus_side, lower_slope, upper_slope, axis_elem, axis_node, direction):
    length = fields.shape[axis_elem]
    slope_minus, slope_plus = face_states(slopes, axis_elem, axis_node, lower_slope, upper_slope)
    face_flux = riemann_flux(minus_side, plus_side, direction) - VISCOSITY * 0.5 * (slope_minus + slope_plus)
    flux_total = physical_flux(fields, direction)[0] - VISCOSITY * slopes
    lower_face = element_range(face_flux, axis_elem, 0, length)
    upper_face = element_range(face_flux, axis_elem, 1, length + 1)
    change = -derivative(flux_total, axis_node)
    lowest = node_layer(change, axis_node, 0) + LIFT_FACTOR * (lower_face - node_layer(flux_total, axis_node, 0))
    middle = node_layer(change, axis_node, 1)
    highest = node_layer(change, axis_node, 2) - LIFT_FACTOR * (upper_face - node_layer(flux_total, axis_node, 2))
    return jnp.concatenate([lowest, middle, highest], axis=axis_node)

def wall_image(trace):
    mirror_signs = jnp.array([1.0, -1.0, -1.0, -1.0, 1.0], dtype=trace.dtype)
    return trace * mirror_signs.reshape((1, 1, 5, 1, 1, 1, 1))

def periodic_traces(values, axis_elem, axis_node):
    length = values.shape[axis_elem]
    lower_trace = node_layer(element_range(values, axis_elem, length - 1, length), axis_node, 2)
    upper_trace = node_layer(element_range(values, axis_elem, 0, 1), axis_node, 0)
    return (lower_trace, upper_trace)

def periodic_rate(fields, axis_elem, axis_node, direction):
    lower_trace, upper_trace = periodic_traces(fields, axis_elem, axis_node)
    minus_side, plus_side = face_states(fields, axis_elem, axis_node, lower_trace, upper_trace)
    slopes = gradient_of(fields, minus_side, plus_side, axis_elem, axis_node)
    lower_slope, upper_slope = periodic_traces(slopes, axis_elem, axis_node)
    return divergence(fields, slopes, minus_side, plus_side, lower_slope, upper_slope, axis_elem, axis_node, direction)

def wall_normal_rate(fields):
    length = fields.shape[1]
    lower_trace = wall_image(node_layer(element_range(fields, 1, 0, 1), 4, 0))
    upper_trace = node_layer(element_range(fields, 1, length - 1, length), 4, 2)
    minus_side, plus_side = face_states(fields, 1, 4, lower_trace, upper_trace)
    slopes = gradient_of(fields, minus_side, plus_side, 1, 4)
    lower_slope = node_layer(element_range(slopes, 1, 0, 1), 4, 0)
    upper_slope = node_layer(element_range(slopes, 1, length - 1, length), 4, 2)
    return divergence(fields, slopes, minus_side, plus_side, lower_slope, upper_slope, 1, 4, 1)

def to_nodes(fields):
    return fields.reshape((fields.shape[0], fields.shape[1], 5, 3, 3, 3, fields.shape[4]))

def to_elements(node_values):
    return node_values.reshape((node_values.shape[0], node_values.shape[1], 5, 27, node_values.shape[6]))

def node_weights():
    ends = jnp.array([1.0 / 3.0, 4.0 / 3.0, 1.0 / 3.0], dtype=jnp.float32)
    return (ends[:, None, None] * ends[None, :, None] * ends[None, None, :]).reshape((27,))

def extension_tables():
    below_rows = np.array([[6.0, -8.0, 3.0], [3.0, -3.0, 1.0], [1.0, 0.0, 0.0]])
    above_rows = np.array([[0.0, 0.0, 1.0], [1.0, -3.0, 3.0], [3.0, -8.0, 6.0]])
    identity_three = np.eye(3)
    inner = np.kron(below_rows, identity_three)
    tables = np.stack([np.kron(above_rows, inner), np.kron(identity_three, inner), np.kron(below_rows, inner)])
    return jnp.asarray(tables, dtype=jnp.float32)

def cut_packs(row_rate, cut_code, cut_rule, rule_fractions, wall_scale):
    rules = rule_fractions.shape[0]
    onehot = (cut_rule[:, None, :] == lax.iota(jnp.int32, rules)[None, :, None]).astype(jnp.float32)
    fractions = jnp.einsum('xrz,rk->xkz', onehot, rule_fractions, precision=lax.Precision.HIGHEST)
    is_cut = cut_code > 0
    weights = node_weights()[None, :, None] * fractions * (is_cut.astype(jnp.float32) * wall_scale)[:, None, :]
    residual = weights[:, None] * row_rate
    packed = jnp.concatenate([residual, weights[:, None]], axis=1)
    code_masks = [(cut_code == code_index).astype(jnp.float32) for code_index in (1, 2, 3)]
    pack_list = [packed * mask_values[:, None, None, :] for mask_values in code_masks]
    return (pack_list, code_masks, is_cut)

def cholesky_solve(matrix, rhs_values):
    order_size = matrix.shape[0]
    row_index = lax.iota(jnp.int32, order_size)
    columns_done = []
    for column in range(order_size):
        current = matrix[:, column]
        if column > 0:
            earlier = jnp.stack(columns_done, axis=1)
            current = current - jnp.einsum('ikxz,kxz->ixz', earlier, earlier[column], precision=lax.Precision.HIGHEST)
        pivot_root = jnp.sqrt(current[column])
        columns_done.append(jnp.where((row_index >= column)[:, None, None], current / pivot_root, 0.0))
    factor = jnp.stack(columns_done, axis=1)
    solved = []
    for position in range(order_size):
        partial_value = rhs_values[:, position]
        if position > 0:
            partial_value = partial_value - jnp.einsum('kxz,vkxz->vxz', factor[position, :position], jnp.stack(solved, axis=1), precision=lax.Precision.HIGHEST)
        solved.append(partial_value / factor[position, position])
    middle = jnp.stack(solved, axis=1)
    result = [None] * order_size
    for position in range(order_size - 1, -1, -1):
        partial_value = middle[:, position]
        if position < order_size - 1:
            partial_value = partial_value - jnp.einsum('kxz,vkxz->vxz', factor[position + 1:, position], jnp.stack(result[position + 1:], axis=1), precision=lax.Precision.HIGHEST)
        result[position] = partial_value / factor[position, position]
    return jnp.stack(result, axis=1)

def merge_solve(row_rate, sources):
    weights = node_weights()
    extension = extension_tables()
    residual = jnp.transpose(weights[None, None, :, None] * row_rate, (1, 2, 0, 3))
    shape_out = (27, 27, row_rate.shape[0], row_rate.shape[3])
    matrix = jnp.broadcast_to(jnp.diag(weights)[:, :, None, None], shape_out)
    for code_index in range(3):
        source = sources[code_index]
        table = extension[code_index]
        residual = residual + jnp.einsum('ia,xviz->vaxz', table, source[:, 0:5], precision=lax.Precision.HIGHEST)
        scaled = table[:, :, None, None] * jnp.transpose(source[:, 5], (1, 0, 2))[:, None]
        matrix = matrix + jnp.einsum('ia,ibxz->abxz', table, scaled, precision=lax.Precision.HIGHEST)
    has_target = sources[0][:, 5, 0] + sources[1][:, 5, 0] + sources[2][:, 5, 0] > 0.0
    solution = cholesky_solve(matrix, residual)
    return (jnp.transpose(solution, (2, 0, 1, 3)), has_target)

def extend_to_cuts(targets, code_masks):
    extension = extension_tables()
    update = code_masks[0][:, None, None, :] * jnp.einsum('ia,xvaz->xviz', extension[0], targets[0], precision=lax.Precision.HIGHEST)
    for code_index in (1, 2):
        update = update + code_masks[code_index][:, None, None, :] * jnp.einsum('ia,xvaz->xviz', extension[code_index], targets[code_index], precision=lax.Precision.HIGHEST)
    return update

def reference(section_start, section_state, cut_code, cut_rule, rule_fractions):
    node_values = to_nodes(section_state)
    tendency = periodic_rate(node_values, 0, 3, 0) + wall_normal_rate(node_values)
    tendency = to_elements(tendency + periodic_rate(node_values, 6, 5, 2))
    pack_list, code_masks, is_cut = cut_packs(tendency[:, 0], cut_code, cut_rule, rule_fractions, 1.0)
    sources = [jnp.roll(pack_list[0], -1, axis=0), pack_list[1], jnp.roll(pack_list[2], 1, axis=0)]
    solution, has_target = merge_solve(tendency[:, 1], sources)
    targets = [jnp.roll(solution, 1, axis=0), solution, jnp.roll(solution, -1, axis=0)]
    cut_update = extend_to_cuts(targets, code_masks)
    wall_row = jnp.where(is_cut[:, None, None, :], cut_update, tendency[:, 0])
    target_row = jnp.where(has_target[:, None, None, :], solution, tendency[:, 1])
    change = jnp.concatenate([wall_row[:, None], target_row[:, None], tendency[:, 2:]], axis=1)
    return 0.75 * section_start + 0.25 * (section_state + TIME_STEP * change)
```

```python
import functools

import jax
import jax.numpy as jnp
from jax import lax
from jax.experimental import pallas as pl
from jax.experimental.pallas import tpu as pltpu
from jax.sharding import PartitionSpec as P

BLOCK = 136
NODES = 27
ROWS_OUT = 160


def swaps(pairs):
    return [p for a, b in pairs for p in ((a, b), (b, a))]


def pack_kernel(state, code, rule, wide_a, wide_b, narrow_a, narrow_b, far):
    w = lax.axis_index("wide")
    n = lax.axis_index("narrow")
    odd = lax.rem(w, 2)
    low_pair = jnp.where(lax.rem(w, 4) < 2, 1, 0)

    def put(target, slot, column, row):
        for v in range(5):
            target[slot * BLOCK + 27 * v : slot * BLOCK + 27 * v + 27, :] = state[column, row, v]

    for target, near in ((wide_a, odd), (wide_b, 1 - odd)):
        for row in range(4):
            put(target, row, near, row)
        for row in range(2):
            put(target, 4 + row, 1 - near, row)
        for slot, table, column in (
            (0, code, near),
            (1, rule, near),
            (4, code, 1 - near),
            (5, rule, 1 - near),
        ):
            line = table[pl.ds(column, 1), :].astype(jnp.float32)
            target[slot * BLOCK + 135 : slot * BLOCK + 136, :] = line
    odd_n = lax.rem(n, 2)
    for column in range(2):
        put(narrow_a, column, column, 3 - 3 * odd_n)
        first = jnp.where(n == 0, low_pair, 0) if column == 0 else 1
        put(narrow_b, column, first, 3 * odd_n)
    put(far, 0, 1 - low_pair, 0)


def flux(v, d):
    inverse = 1.0 / v[0]
    speed = v[1 + d] * inverse
    kinetic = v[1] * v[1] + v[2] * v[2] + v[3] * v[3]
    pressure = 0.4 * (v[4] - 0.5 * kinetic * inverse)
    return own_flux(v, d, inverse, pressure), jnp.abs(speed) + jnp.sqrt(1.4 * pressure * inverse)


def own_flux(v, d, inverse, pressure):
    speed = v[1 + d] * inverse
    out = [v[1 + d], v[1] * speed, v[2] * speed, v[3] * speed, (v[4] + pressure) * speed]
    out[1 + d] = out[1 + d] + pressure
    return out


def slope_low(v):
    return [-1.5 * a + 2.0 * b - 0.5 * c for a, b, c in zip(*v)]


def slope_high(v):
    return [0.5 * a - 2.0 * b + 1.5 * c for a, b, c in zip(*v)]


def line_rate(v, pre, d, low, high, low_slope, high_slope, minus, minus_slope, plus, plus_slope):
    fluxes = [own_flux(v[k], d, pre[k][0], pre[k][1]) for k in range(3)]
    speed_low = jnp.abs(low[1 + d] * pre[0][0]) + pre[0][2]
    speed_high = jnp.abs(high[1 + d] * pre[2][0]) + pre[2][2]
    flux_minus, speed_minus = flux(minus, d)
    flux_plus, speed_plus = flux(plus, d)
    half_low = 0.5 * jnp.maximum(speed_low, speed_minus)
    half_high = 0.5 * jnp.maximum(speed_high, speed_plus)
    first, second, third = [], [], []
    for i in range(5):
        jump_low = low[i] - minus[i]
        jump_high = plus[i] - high[i]
        lift_low = 1.5 * jump_low
        lift_high = 1.5 * jump_high
        q_low = low_slope[i] + lift_low
        q_high = high_slope[i] + lift_high
        face_low = (
            0.5 * (flux_minus[i] + fluxes[0][i])
            - half_low * jump_low
            - 0.05 * (minus_slope[i] + lift_low + q_low)
        )
        face_high = (
            0.5 * (fluxes[2][i] + flux_plus[i])
            - half_high * jump_high
            - 0.05 * (plus_slope[i] + lift_high + q_high)
        )
        g_low = fluxes[0][i] - 0.1 * q_low
        g_mid = fluxes[1][i] - 0.05 * (high[i] - low[i])
        g_high = fluxes[2][i] - 0.1 * q_high
        first.append(3.0 * face_low - 1.5 * g_low - 2.0 * g_mid + 0.5 * g_high)
        second.append(0.5 * (g_low - g_high))
        third.append(-3.0 * face_high - 0.5 * g_low + 2.0 * g_mid + 1.5 * g_high)
    return first, second, third


def load(ref, node):
    return [ref[i, node] for i in range(5)]


def prepare(blocks, nodes, pre):
    def body(n, carry):
        v = []
        for i in range(5):
            value = blocks[pl.ds(27 * i + n, 8, stride=BLOCK), :]
            nodes[i, n] = value
            v.append(value)
        if pre is not None:
            inverse = 1.0 / v[0]
            kinetic = v[1] * v[1] + v[2] * v[2] + v[3] * v[3]
            pressure = 0.4 * (v[4] - 0.5 * kinetic * inverse)
            pre[0, n] = inverse
            pre[1, n] = pressure
            pre[2, n] = jnp.sqrt(1.4 * pressure * inverse)
        return carry

    lax.fori_loop(0, NODES, body, 0)


def sweep(nodes, pre, rate, d, neighbours):
    step = (9, 3, 1)[d]

    def body(line, carry):
        base = (line, 9 * (line // 3) + lax.rem(line, 3), 3 * line)[d]
        at = [base + step * k for k in range(3)]
        v = [load(nodes, n) for n in at]
        p = [[pre[j, n] for j in range(3)] for n in at]
        low_slope, high_slope = slope_low(v), slope_high(v)
        traces = neighbours(at, v, low_slope, high_slope)
        parts = line_rate(v, p, d, v[0], v[2], low_slope, high_slope, *traces)
        for k in range(3):
            for i in range(5):
                if d == 0:
                    rate[i, at[k]] = parts[k][i]
                else:
                    rate[i, at[k]] += parts[k][i]
        return carry

    lax.fori_loop(0, 9, body, 0)


def roll(x, shift):
    return pltpu.roll(x, shift % 8, 0)


def span_neighbours(at, v, low_slope, high_slope):
    before = [pltpu.roll(x, 1, 1) for x in v[2]]
    before_slope = [pltpu.roll(x, 1, 1) for x in high_slope]
    after = [pltpu.roll(x, 127, 1) for x in v[0]]
    after_slope = [pltpu.roll(x, 127, 1) for x in low_slope]
    return before, before_slope, after, after_slope


def mirrored(v):
    return [v[0], -v[1], -v[2], -v[3], v[4]]


def halo_trace(halo, at, lower):
    u = [[halo[pl.ds(27 * i + n, 8, stride=BLOCK), :] for i in range(5)] for n in at]
    near = [jnp.where(lower, c, a) for a, c in zip(u[0], u[2])]
    away = [jnp.where(lower, a, c) for a, c in zip(u[0], u[2])]
    slope = [1.5 * a - 2.0 * b + 0.5 * c for a, b, c in zip(near, u[1], away)]
    return near, [jnp.where(lower, s, -s) for s in slope]


def main_rate(own, halo_x, halo_y, nodes, pre, rate, at_bottom, at_top):
    sub = lax.broadcasted_iota(jnp.int32, (8, 128), 0)
    first_column = sub < 4
    height = lax.rem(sub, 4)
    lowest, highest = height == 0, height == 3
    wall, top = jnp.logical_and(lowest, at_bottom), jnp.logical_and(highest, at_top)

    def flow(at, v, low_slope, high_slope):
        halo, halo_slope = halo_trace(halo_x, at, first_column)
        minus = [jnp.where(first_column, h, roll(x, 4)) for h, x in zip(halo, v[2])]
        minus_slope = [jnp.where(first_column, h, roll(x, 4)) for h, x in zip(halo_slope, high_slope)]
        plus = [jnp.where(first_column, roll(x, 4), h) for h, x in zip(halo, v[0])]
        plus_slope = [jnp.where(first_column, roll(x, 4), h) for h, x in zip(halo_slope, low_slope)]
        return minus, minus_slope, plus, plus_slope

    def normal(at, v, low_slope, high_slope):
        halo, halo_slope = halo_trace(halo_y, at, lowest)

        def pick(edge, other, h, inside, x, shift):
            return jnp.where(other, inside, jnp.where(edge, h, roll(x, shift)))

        minus = [pick(lowest, wall, h, m, x, 1) for h, m, x in zip(halo, mirrored(v[0]), v[2])]
        minus_slope = [
            pick(lowest, wall, h, s, x, 1) for h, s, x in zip(halo_slope, low_slope, high_slope)
        ]
        plus = [pick(highest, top, h, m, x, -1) for h, m, x in zip(halo, v[2], v[0])]
        plus_slope = [
            pick(highest, top, h, s, x, -1) for h, s, x in zip(halo_slope, high_slope, low_slope)
        ]
        return minus, minus_slope, plus, plus_slope

    prepare(own, nodes, pre)
    sweep(nodes, pre, rate, 0, flow)
    sweep(nodes, pre, rate, 1, normal)
    sweep(nodes, pre, rate, 2, span_neighbours)


def strip_rates(groups, nodes, pre, rate):
    for g in range(3):
        prepare(groups[g], nodes.at[g], pre.at[g] if g < 2 else None)

    def flow(at, v, low_slope, high_slope):
        return (
            [roll(x, 1) for x in v[2]],
            [roll(x, 1) for x in high_slope],
            [roll(x, -1) for x in v[0]],
            [roll(x, -1) for x in low_slope],
        )

    for g in range(2):

        def normal(at, v, low_slope, high_slope, g=g):
            above = [load(nodes.at[g + 1], n) for n in at]
            if g == 0:
                minus, minus_slope = mirrored(v[0]), low_slope
            else:
                below = [load(nodes.at[0], n) for n in at]
                minus, minus_slope = below[2], slope_high(below)
            return minus, minus_slope, above[0], slope_low(above)

        sweep(nodes.at[g], pre.at[g], rate.at[g], 0, flow)
        sweep(nodes.at[g], pre.at[g], rate.at[g], 1, normal)
        sweep(nodes.at[g], pre.at[g], rate.at[g], 2, span_neighbours)


def below_rows(x):
    return [6.0 * x[0] - 8.0 * x[1] + 3.0 * x[2], 3.0 * x[0] - 3.0 * x[1] + x[2], x[0]]


def above_rows(x):
    return [x[2], x[0] - 3.0 * x[1] + 3.0 * x[2], 3.0 * x[0] - 8.0 * x[1] + 6.0 * x[2]]


def below_columns(x):
    return [6.0 * x[0] + 3.0 * x[1] + x[2], -8.0 * x[0] - 3.0 * x[1], 3.0 * x[0] + x[1]]


def above_columns(x):
    return [x[1] + 3.0 * x[2], -3.0 * x[1] - 8.0 * x[2], x[0] + 3.0 * x[1] + 6.0 * x[2]]


BELOW = ((6.0, -8.0, 3.0), (3.0, -3.0, 1.0), (1.0, 0.0, 0.0))
ABOVE = ((0.0, 0.0, 1.0), (1.0, -3.0, 3.0), (3.0, -8.0, 6.0))
ENDS = (1.0 / 3.0, 4.0 / 3.0, 1.0 / 3.0)
PAIRS = tuple((i, j) for i in range(3) for j in range(i + 1))


def weight(a, b, c):
    return ENDS[a] * ENDS[b] * ENDS[c]


def combine(table, x, i, j):
    total = None
    for k in range(3):
        factor = table[k][i] * table[k][j]
        if factor != 0.0:
            term = x[k] if factor == 1.0 else factor * x[k]
            total = term if total is None else total + term
    return total


def cut_solve(groups, fractions, taken, nodes, rate, scaled, right, out):
    code = groups[0][pl.ds(135, 8, stride=BLOCK), :]
    rule = groups[1][pl.ds(135, 8, stride=BLOCK), :]
    index = lax.broadcasted_iota(jnp.int32, (64, 128), 0).astype(jnp.float32)
    onehot = jnp.concatenate(
        [(index == rule[j : j + 1, :]).astype(jnp.float32) for j in range(8)], axis=1
    )
    shares = lax.dot_general(
        fractions[...],
        onehot,
        (((0,), (0,)), ((), ())),
        precision=lax.Precision.HIGHEST,
        preferred_element_type=jnp.float32,
    )
    for j in range(8):
        taken[32 * j : 32 * j + 27, :] = shares[:, 128 * j : 128 * j + 128]
    is_cut = code > 0.0
    cut = is_cut.astype(jnp.float32)
    masks = [(code == float(k)).astype(jnp.float32) for k in (1, 2, 3)]

    def source_of(x, k):
        return (roll(x, -1), x, roll(x, 1))[k]

    for a in range(3):
        for b in range(3):
            for c in range(3):
                n = 9 * a + 3 * b + c
                amount = weight(a, b, c) * taken[pl.ds(n, 8, stride=32), :] * cut
                for k in range(3):
                    scaled[k, n] = source_of(jnp.where(masks[k] > 0.0, amount, 0.0), k)
                scaled[3, n] = amount
    has_target = source_of(masks[0], 0) + masks[1] + source_of(masks[2], 2) > 0.0

    def right_side(i, carry):
        for c in range(3):
            y = []
            for a in range(3):
                at = [9 * a + 3 * b + c for b in range(3)]
                y.append(below_columns([scaled[3, n] * rate[0, i, n] for n in at]))
            for b in range(3):
                x = [y[a][b] for a in range(3)]
                parts = (above_columns(x), x, below_columns(x))
                for a in range(3):
                    n = 9 * a + 3 * b + c
                    total = weight(a, b, c) * rate[1, i, n]
                    for k in range(3):
                        total += source_of(jnp.where(masks[k] > 0.0, parts[k][a], 0.0), k)
                    right[i, n] = total
        return carry

    lax.fori_loop(0, 5, right_side, 0)

    for c in range(3):
        inner = []
        for k in range(3):
            per_a = []
            for a in range(3):
                x = [scaled[k, 9 * a + 3 * b + c] for b in range(3)]
                per_a.append({p: combine(BELOW, x, *p) for p in PAIRS})
            inner.append(per_a)
        matrix = {}
        for a, b in ((a, b) for a in range(3) for b in range(3)):
            for a2, b2 in ((a2, b2) for a2 in range(3) for b2 in range(3)):
                row, column = 3 * a + b, 3 * a2 + b2
                if column > row:
                    continue
                p = (max(b, b2), min(b, b2))
                total = combine(ABOVE, [inner[0][i][p] for i in range(3)], a, a2)
                third = combine(BELOW, [inner[2][i][p] for i in range(3)], a, a2)
                if third is not None:
                    total = third if total is None else total + third
                if a == a2:
                    total = total + inner[1][a][p]
                if row == column:
                    total = total + weight(a, b, c)
                matrix[row, column] = total
        place = [9 * (r // 3) + 3 * (r % 3) + c for r in range(9)]
        inverse, lower = [], {}
        for j in range(9):
            inverse.append(1.0 / matrix[j, j])
            for r in range(j + 1, 9):
                lower[r, j] = matrix[r, j] * inverse[j]
            for r in range(j + 1, 9):
                for s in range(j + 1, r + 1):
                    matrix[r, s] = matrix[r, s] - lower[r, j] * matrix[s, j]
        for i in range(5):
            x = [right[i, n] for n in place]
            for j in range(9):
                for r in range(j + 1, 9):
                    x[r] = x[r] - lower[r, j] * x[j]
            x = [x[j] * inverse[j] for j in range(9)]
            for j in range(8, -1, -1):
                for r in range(j):
                    x[r] = x[r] - lower[j, r] * x[j]
            for j in range(9):
                right[i, place[j]] = x[j]

    def finish(i, carry):
        for c in range(3):
            y = []
            for a in range(3):
                x = []
                for b in range(3):
                    s = right[i, 9 * a + 3 * b + c]
                    x.append(
                        jnp.where(masks[0] > 0.0, roll(s, 1), jnp.where(masks[2] > 0.0, roll(s, -1), s))
                    )
                y.append(below_rows(x))
            for b in range(3):
                x = [y[a][b] for a in range(3)]
                one, three = above_rows(x), below_rows(x)
                for a in range(3):
                    n = 9 * a + 3 * b + c
                    update = jnp.where(masks[0] > 0.0, one[a], jnp.where(masks[2] > 0.0, three[a], x[a]))
                    change = jnp.where(is_cut, update, rate[0, i, n])
                    value = 0.25 * (nodes[0, i, n] + 0.03 * change)
                    out[pl.ds(32 * i + n, 2, stride=4 * ROWS_OUT), :] = value[3:5]
                    change = jnp.where(has_target, right[i, n], rate[1, i, n])
                    value = 0.25 * (nodes[1, i, n] + 0.03 * change)
                    out[pl.ds(ROWS_OUT + 32 * i + n, 2, stride=4 * ROWS_OUT), :] = value[3:5]
        return carry

    lax.fori_loop(0, 5, finish, 0)


def rate_kernel(
    start,
    mine_a,
    mine_b,
    wide_a,
    wide_b,
    narrow_a,
    narrow_b,
    far,
    fractions,
    out,
    start_v,
    own,
    halo_x,
    halo_y,
    row0,
    row1,
    row2,
    nodes,
    pre,
    rate,
    strip_nodes,
    strip_pre,
    strip_rate,
    taken,
    scaled,
    right,
    staged,
    sem,
    strip_sem,
):
    w = lax.axis_index("wide")
    n = lax.axis_index("narrow")
    odd, odd_n = lax.rem(w, 2), lax.rem(n, 2)
    low_pair = lax.rem(w, 4) < 2
    at_bottom, at_top = n == 0, n == lax.axis_size("narrow") - 1

    def rows(first, count):
        return pl.ds(first * BLOCK, count * BLOCK)

    def slots(first, count):
        return pl.ds(pl.multiple_of(first * BLOCK, 8), count * BLOCK)

    low_y, high_y = 3 - 3 * odd_n, 3 * odd_n
    moves = [
        (mine_a.at[rows(0, 4)], own.at[slots(4 * odd, 4)]),
        (mine_b.at[rows(0, 4)], own.at[slots(4 - 4 * odd, 4)]),
        (wide_a.at[rows(0, 4)], halo_x.at[slots(4 * odd, 4)]),
        (wide_b.at[rows(0, 4)], halo_x.at[slots(4 - 4 * odd, 4)]),
        (narrow_a.at[rows(0, 1)], halo_y.at[slots(low_y, 1)]),
        (narrow_a.at[rows(1, 1)], halo_y.at[slots(low_y + 4, 1)]),
        (narrow_b.at[rows(0, 1)], halo_y.at[slots(high_y, 1)]),
        (narrow_b.at[rows(1, 1)], halo_y.at[slots(high_y + 4, 1)]),
        (start, start_v),
    ]
    copies = [pltpu.make_async_copy(a, b, sem.at[i]) for i, (a, b) in enumerate(moves)]
    for copy in copies:
        copy.start()

    near, away = jnp.where(odd == 1, 5, 2), jnp.where(odd == 1, 6, 1)
    mine = 3 + odd
    strips = [
        (wide_a.at[rows(0, 1)], row0.at[slots(near, 1)]),
        (wide_a.at[rows(4, 1)], row0.at[slots(away, 1)]),
        (wide_a.at[rows(1, 1)], row1.at[slots(near, 1)]),
        (wide_a.at[rows(5, 1)], row1.at[slots(away, 1)]),
        (wide_a.at[rows(2, 1)], row2.at[slots(near, 1)]),
        (wide_b.at[rows(0, 1)], row0.at[slots(7 - near, 1)]),
        (wide_b.at[rows(4, 1)], row0.at[slots(7 - away, 1)]),
        (wide_b.at[rows(1, 1)], row1.at[slots(7 - near, 1)]),
        (wide_b.at[rows(5, 1)], row1.at[slots(7 - away, 1)]),
        (wide_b.at[rows(2, 1)], row2.at[slots(7 - near, 1)]),
        (mine_a.at[rows(0, 1)], row0.at[slots(mine, 1)]),
        (mine_a.at[rows(1, 1)], row1.at[slots(mine, 1)]),
        (mine_a.at[rows(2, 1)], row2.at[slots(mine, 1)]),
        (mine_b.at[rows(0, 1)], row0.at[slots(7 - mine, 1)]),
        (mine_b.at[rows(1, 1)], row1.at[slots(7 - mine, 1)]),
        (mine_b.at[rows(2, 1)], row2.at[slots(7 - mine, 1)]),
        (narrow_b.at[rows(0, 1)], row0.at[slots(jnp.where(low_pair, 7, 0), 1)]),
        (far.at[rows(0, 1)], row0.at[slots(jnp.where(low_pair, 0, 7), 1)]),
    ]
    strip_copies = [
        pltpu.make_async_copy(a, b, strip_sem.at[i]) for i, (a, b) in enumerate(strips)
    ]

    @pl.when(at_bottom)
    def _():
        for copy in strip_copies:
            copy.start()

    for copy in copies[:8]:
        copy.wait()
    main_rate(own, halo_x, halo_y, nodes, pre, rate, at_bottom, at_top)

    def stage(node, carry):
        for i in range(5):
            value = 0.25 * (nodes[i, node] + 0.03 * rate[i, node])
            staged[pl.ds(32 * i + node, 8, stride=ROWS_OUT), :] = value
        return carry

    lax.fori_loop(0, NODES, stage, 0)

    @pl.when(at_bottom)
    def _():
        for copy in strip_copies:
            copy.wait()
        groups = (row0, row1, row2)
        strip_rates(groups, strip_nodes, strip_pre, strip_rate)
        cut_solve(groups, fractions, taken, strip_nodes, strip_rate, scaled, right, staged)

    copies[8].wait()
    for x in range(2):
        for y in range(4):
            for i in range(5):
                first = (4 * x + y) * ROWS_OUT + 32 * i
                out[x, y, i] = 0.75 * start_v[x, y, i] + staged[first : first + 27, :]


def device_step(wide, narrow, section_start, section_state, cut_code, cut_rule, rule_fractions):
    vmem = pl.BlockSpec(memory_space=pltpu.VMEM)
    anywhere = pl.BlockSpec(memory_space=pl.ANY)
    f32 = jnp.float32
    mine_a, mine_b, up_a, up_b, far = pl.pallas_call(
        pack_kernel,
        name="pack",
        out_shape=[
            jax.ShapeDtypeStruct((6 * BLOCK, 128), f32),
            jax.ShapeDtypeStruct((6 * BLOCK, 128), f32),
            jax.ShapeDtypeStruct((2 * BLOCK, 128), f32),
            jax.ShapeDtypeStruct((2 * BLOCK, 128), f32),
            jax.ShapeDtypeStruct((BLOCK, 128), f32),
        ],
        in_specs=[vmem] * 3,
        out_specs=[vmem] * 5,
        compiler_params=pltpu.CompilerParams(vmem_limit_bytes=16 * 2**20),
    )(section_state, cut_code, cut_rule)

    both = ("wide", "narrow")
    cross = swaps([(2 * j + 1, (2 * j + 2) % wide) for j in range(wide // 2)])
    inside = swaps([(2 * j, 2 * j + 1) for j in range(wide // 2)])
    even = swaps([(2 * j, 2 * j + 1) for j in range(narrow // 2)])
    between = [(2 * j + 1, 2 * j + 2) for j in range(narrow // 2 - 1)]
    far_inside = [(4 * j + k, 4 * j + 2 + k) for j in range(wide // 4) for k in (0, 1)]
    far_cross = [(4 * j + 2 + k, (4 * j + 4 + k) % wide) for j in range(wide // 4) for k in (0, 1)]
    mixed = [(narrow * i + a, narrow * i + b) for i in range(wide) for a, b in between]
    mixed = swaps(mixed + [(narrow * a, narrow * b) for a, b in far_inside])
    far_cross = swaps([(narrow * a, narrow * b) for a, b in far_cross])

    got_narrow_a = lax.ppermute(up_a, "narrow", even)
    got_narrow_b = lax.ppermute(up_b, both, mixed)
    got_far = lax.ppermute(far, both, far_cross)
    got_wide_a = lax.ppermute(mine_a, "wide", cross)
    got_wide_b = lax.ppermute(mine_b, "wide", inside)

    blocks = pltpu.VMEM((8 * BLOCK, 128), f32)
    return pl.pallas_call(
        rate_kernel,
        name="rate",
        out_shape=jax.ShapeDtypeStruct(section_start.shape, f32),
        in_specs=[anywhere] * 8 + [vmem],
        out_specs=vmem,
        scratch_shapes=[
            pltpu.VMEM(section_start.shape, f32),
            blocks,
            blocks,
            blocks,
            blocks,
            blocks,
            blocks,
            pltpu.VMEM((5, NODES, 8, 128), f32),
            pltpu.VMEM((3, NODES, 8, 128), f32),
            pltpu.VMEM((5, NODES, 8, 128), f32),
            pltpu.VMEM((3, 5, NODES, 8, 128), f32),
            pltpu.VMEM((2, 3, NODES, 8, 128), f32),
            pltpu.VMEM((2, 5, NODES, 8, 128), f32),
            pltpu.VMEM((8 * 32, 128), f32),
            pltpu.VMEM((4, NODES, 8, 128), f32),
            pltpu.VMEM((5, NODES, 8, 128), f32),
            pltpu.VMEM((8 * ROWS_OUT, 128), f32),
            pltpu.SemaphoreType.DMA((9,)),
            pltpu.SemaphoreType.DMA((18,)),
        ],
        compiler_params=pltpu.CompilerParams(vmem_limit_bytes=32 * 2**20),
    )(
        section_start,
        mine_a,
        mine_b,
        got_wide_a,
        got_wide_b,
        got_narrow_a,
        got_narrow_b,
        got_far,
        rule_fractions,
    )


def solution(mesh):
    return jax.shard_map(
        functools.partial(device_step, mesh.shape["wide"], mesh.shape["narrow"]),
        mesh=mesh,
        in_specs=(
            P("wide", "narrow", None, None, None),
            P("wide", "narrow", None, None, None),
            P("wide", None),
            P("wide", None),
            P(),
        ),
        out_specs=P("wide", "narrow", None, None, None),
        check_vma=False,
    )
```

```python
import functools

import jax
import jax.numpy as jnp
from jax import lax
from jax.experimental import pallas as pl
from jax.experimental.pallas import tpu as pltpu
from jax.sharding import PartitionSpec as P

NODES = 27
COLUMN = 5 * NODES
HALF = 68
WIDE_TILES = COLUMN + HALF + 1
NARROW_TILES = 45
FAR_TILES = 47


def swaps(pairs):
    return [p for a, b in pairs for p in ((a, b), (b, a))]


def nodes_of(line, d):
    base = (line, 9 * (line // 3) + line % 3, 3 * line)[d]
    return [base + (9, 3, 1)[d] * k for k in range(3)]


def sublane():
    return lax.broadcasted_iota(jnp.int32, (8, 128), 0)


def roll(x, shift):
    return pltpu.roll(x, shift % 8, 0)


def edge_slope(near, middle, away):
    return 1.5 * near - 2.0 * middle + 0.5 * away


def pack_wide(state, tables, wide_a, wide_b):
    odd = lax.rem(lax.axis_index("wide"), 2)
    for target, near in ((wide_a, odd), (wide_b, 1 - odd)):
        first, other = near * COLUMN, (1 - near) * COLUMN
        target[0:COLUMN] = state[pl.ds(first, COLUMN)]
        for m in range(HALF):
            later = min(m + HALF, COLUMN - 1)
            target[COLUMN + m, 0:2, :] = state[other + m, 0:2, :]
            target[COLUMN + m, 2:4, :] = state[other + later, 0:2, :]
        own, swapped = tables[...], jnp.concatenate([tables[2:4], tables[0:2]], axis=0)
        target[WIDE_TILES - 1] = jnp.where(near == 0, own, swapped)


def pack_rest(state, far, narrow_a, narrow_b):
    w, n = lax.axis_index("wide"), lax.axis_index("narrow")
    low_pair = lax.rem(w, 4) < 2
    odd_n, lowest = lax.rem(n, 2) == 1, n == 0

    def edge(column, i, line, d, high):
        at = [27 * i + k for k in nodes_of(line, d)]
        if column is None:
            u = [jnp.concatenate([state[k], state[COLUMN + k]], axis=0) for k in at]
        else:
            u = [state[column * COLUMN + k] for k in at]
        near, away = jnp.where(high, u[2], u[0]), jnp.where(high, u[0], u[2])
        slope = edge_slope(near, u[1], away)
        return near, jnp.where(high, slope, -slope)

    for i in range(5):
        for line in range(9):
            m = 9 * i + line
            near, slope = edge(1 - low_pair.astype(jnp.int32), i, line, 0, jnp.logical_not(low_pair))
            far[m, 0:1, :] = near[0:1]
            far[m, 2:3, :] = slope[0:1]
            wall_near, wall_slope = edge(low_pair.astype(jnp.int32), i, line, 0, low_pair)
            for target, high, wall in (
                (narrow_a, jnp.logical_not(odd_n), False),
                (narrow_b, odd_n, True),
            ):
                near, slope = edge(None, i, line, 1, high)
                for row, x, w_x in ((0, near, wall_near), (2, slope, wall_slope)):
                    first = jnp.where(high, x[3:4], x[0:1])
                    if wall:
                        first = jnp.where(lowest, w_x[0:1], first)
                    target[m, row : row + 1, :] = first
                    target[m, row + 1 : row + 2, :] = jnp.where(high, x[7:8], x[4:5])


def pressure_of(v, inverse):
    return 0.4 * (v[4] - 0.5 * (v[1] * v[1] + v[2] * v[2] + v[3] * v[3]) * inverse)


def flux(v, d, inverse, pressure, sound):
    speed = v[1 + d] * inverse
    out = [v[1 + d], v[1] * speed, v[2] * speed, v[3] * speed, (v[4] + pressure) * speed]
    out[1 + d] = out[1 + d] + pressure
    return out, jnp.abs(speed) + sound


def thermo(v):
    inverse = 1.0 / v[0]
    pressure = pressure_of(v, inverse)
    return inverse, pressure, jnp.sqrt(1.4 * pressure * inverse)


def load(ref, node):
    return [ref[i, node] for i in range(5)]


def fill(vector, nodes, pre):
    for n in range(NODES):
        v = [vector(27 * i + n) for i in range(5)]
        for i in range(5):
            nodes[i, n] = v[i]
        for j, x in enumerate(thermo(v)):
            pre[j, n] = x


def interior(nodes, pre, rate, height):
    sub = sublane()
    inner_x = lax.rem(sub, 2 * height) >= height
    inner_y = lax.rem(sub, height) > 0
    moves = (
        (lambda x: roll(x, height), lambda x: roll(x, -height), inner_x),
        (lambda x: roll(x, 1), lambda x: roll(x, -1), inner_y),
        (lambda x: pltpu.roll(x, 1, 1), lambda x: pltpu.roll(x, 127, 1), None),
    )
    for d in range(3):
        ahead, back, inner = moves[d]

        def body(line, carry, d=d, ahead=ahead, back=back, inner=inner):
            base = (line, 9 * (line // 3) + lax.rem(line, 3), 3 * line)[d]
            at = [base + (9, 3, 1)[d] * k for k in range(3)]
            v = [load(nodes, n) for n in at]
            f, speeds = zip(*[flux(v[k], d, *[pre[j, at[k]] for j in range(3)]) for k in range(3)])
            speed = 0.5 * jnp.maximum(speeds[0], ahead(speeds[2]))
            for i in range(5):
                a, b, c = v[0][i], v[1][i], v[2][i]
                g_low = f[0][i] + 0.1 * edge_slope(a, b, c)
                g_mid = f[1][i] - 0.05 * (c - a)
                g_high = f[2][i] - 0.1 * edge_slope(c, b, a)
                jump = a - ahead(c)
                lift = 0.075 * jump
                face = 1.5 * (ahead(g_high) + g_low) - 3.0 * (speed * jump) - 3.0 * lift
                if inner is not None:
                    face, lift = jnp.where(inner, face, 0.0), jnp.where(inner, lift, 0.0)
                face_up, lift_up = back(face), back(lift)
                first = face - lift_up - 1.5 * g_low - 2.0 * g_mid + 0.5 * g_high
                second = lift_up - lift + 0.5 * (g_low - g_high)
                third = lift - face_up - 0.5 * g_low + 2.0 * g_mid + 1.5 * g_high
                for n, x in zip(at, (first, second, third)):
                    rate[i, n] = x if d == 0 else rate[i, n] + x
            return carry

        lax.fori_loop(0, 9, body, 0)


def outer(nodes, rate, d, lower, active, halo):
    turn = jnp.where(lower, 1.0, -1.0)
    for line in range(9):
        at = nodes_of(line, d)
        v = [load(nodes, n) for n in at]
        near = [jnp.where(lower, a, c) for a, c in zip(v[0], v[2])]
        away = [jnp.where(lower, c, a) for a, c in zip(v[0], v[2])]
        slope = [-turn * edge_slope(*x) for x in zip(near, v[1], away)]
        other, other_slope = halo(line, near, slope)
        f, speed = flux(near, d, *thermo(near))
        f_other, speed_other = flux(other, d, *thermo(other))
        half = 0.5 * jnp.maximum(speed, speed_other)
        for i in range(5):
            jump = turn * (near[i] - other[i])
            face = (
                0.5 * (f[i] + f_other[i])
                - half * jump
                - 0.05 * (slope[i] + other_slope[i])
                - 0.15 * jump
            )
            edge = jnp.where(active, turn * (3.0 * face + 0.225 * jump), 0.0)
            lift = jnp.where(active, turn * (0.075 * jump), 0.0)
            rate[i, at[0]] += jnp.where(lower, edge, lift)
            rate[i, at[1]] -= lift
            rate[i, at[2]] += jnp.where(lower, lift, edge)


def mirrored(v):
    return [v[0], -v[1], -v[2], -v[3], v[4]]


def inner_kernel(state, nodes, rate, pre):
    fill(lambda k: jnp.concatenate([state[k], state[COLUMN + k]], axis=0), nodes, pre)
    interior(nodes, pre, rate, 4)


def below_rows(x):
    return [6.0 * x[0] - 8.0 * x[1] + 3.0 * x[2], 3.0 * x[0] - 3.0 * x[1] + x[2], x[0]]


def above_rows(x):
    return [x[2], x[0] - 3.0 * x[1] + 3.0 * x[2], 3.0 * x[0] - 8.0 * x[1] + 6.0 * x[2]]


def below_columns(x):
    return [6.0 * x[0] + 3.0 * x[1] + x[2], -8.0 * x[0] - 3.0 * x[1], 3.0 * x[0] + x[1]]


def above_columns(x):
    return [x[1] + 3.0 * x[2], -3.0 * x[1] - 8.0 * x[2], x[0] + 3.0 * x[1] + 6.0 * x[2]]


BELOW = ((6.0, -8.0, 3.0), (3.0, -3.0, 1.0), (1.0, 0.0, 0.0))
ABOVE = ((0.0, 0.0, 1.0), (1.0, -3.0, 3.0), (3.0, -8.0, 6.0))
ENDS = (1.0 / 3.0, 4.0 / 3.0, 1.0 / 3.0)
PAIRS = tuple((i, j) for i in range(3) for j in range(i + 1))
BELOW_DIAGONAL = tuple((r, j) for j in range(9) for r in range(j + 1, 9))


def weight(a, b, c):
    return ENDS[a] * ENDS[b] * ENDS[c]


def combine(table, x, i, j):
    total = None
    for k in range(3):
        factor = table[k][i] * table[k][j]
        if factor != 0.0:
            term = x[k] if factor == 1.0 else factor * x[k]
            total = term if total is None else total + term
    return total


def source_of(x, k):
    return (roll(x, -1), x, roll(x, 1))[k]


def masks_of(code):
    return [(code == float(k)).astype(jnp.float32) for k in (1, 2, 3)]


def factorize(code, rule, fractions, taken, scaled, factor):
    index = lax.broadcasted_iota(jnp.int32, (64, 128), 0).astype(jnp.float32)
    onehot = jnp.concatenate(
        [(index == rule[j : j + 1, :]).astype(jnp.float32) for j in range(8)], axis=1
    )
    shares = lax.dot_general(
        fractions[...],
        onehot,
        (((1,), (0,)), ((), ())),
        precision=lax.Precision.HIGHEST,
        preferred_element_type=jnp.float32,
    )
    for j in range(8):
        taken[32 * j : 32 * j + 27, :] = shares[:, 128 * j : 128 * j + 128]
    is_cut = code > 0.0
    masks = masks_of(code)
    for c in range(3):
        inner = [[None] * 3 for _ in range(3)]
        for a in range(3):
            parts = [[], [], []]
            for b in range(3):
                n = 9 * a + 3 * b + c
                amount = jnp.where(is_cut, weight(a, b, c) * taken[pl.ds(n, 8, stride=32), :], 0.0)
                scaled[n] = amount
                for k in range(3):
                    parts[k].append(source_of(jnp.where(masks[k] > 0.0, amount, 0.0), k))
            for k in range(3):
                inner[k][a] = {p: combine(BELOW, parts[k], *p) for p in PAIRS}
        matrix = {}
        for row in range(9):
            for column in range(row + 1):
                (a, b), (a2, b2) = divmod(row, 3), divmod(column, 3)
                p = (max(b, b2), min(b, b2))
                total = combine(ABOVE, [inner[0][i][p] for i in range(3)], a, a2)
                third = combine(BELOW, [inner[2][i][p] for i in range(3)], a, a2)
                if third is not None:
                    total = third if total is None else total + third
                if a == a2:
                    total = total + inner[1][a][p]
                if row == column:
                    total = total + weight(a, b, c)
                matrix[row, column] = total
        for j in range(9):
            inverse = 1.0 / matrix[j, j]
            factor[c, 36 + j] = inverse
            lower = {r: matrix[r, j] * inverse for r in range(j + 1, 9)}
            for r in range(j + 1, 9):
                factor[c, BELOW_DIAGONAL.index((r, j))] = lower[r]
                for s in range(j + 1, r + 1):
                    matrix[r, s] = matrix[r, s] - lower[r] * matrix[s, j]


def edge_kernel(
    nodes,
    rate_in,
    wide_a,
    wide_b,
    narrow_a,
    narrow_b,
    tables,
    fractions,
    rate,
    strip_nodes,
    strip_rate,
    codes,
    scaled,
    factor,
    taken,
    strip_pre,
):
    rate[...] = rate_in[...]
    odd = lax.rem(lax.axis_index("wide"), 2) == 1
    n = lax.axis_index("narrow")
    odd_n, at_bottom, at_top = lax.rem(n, 2) == 1, n == 0, n == lax.axis_size("narrow") - 1
    sub = sublane()
    first_column = sub < 4
    height = lax.rem(sub, 4)

    def sides(k):
        a, b = wide_a[k], wide_b[k]
        return jnp.where(odd, b, a), jnp.where(odd, a, b)

    def both_sides(k_left, k_right):
        return jnp.concatenate([sides(k_left)[0], sides(k_right)[1]], axis=0)

    def across(line, near, slope):
        at = nodes_of(line, 0)
        u = [
            [both_sides(27 * i + at[2 - j], 27 * i + at[j]) for i in range(5)] for j in range(3)
        ]
        other = [edge_slope(*x) for x in zip(*u)]
        return u[0], [jnp.where(first_column, x, -x) for x in other]

    lowest = height == 0
    wall = jnp.logical_and(lowest, at_bottom)
    top = jnp.logical_and(height == 3, at_top)

    def upright(line, near, slope):
        other, other_slope = [], []
        image = mirrored(near)
        for i in range(5):
            a, b = narrow_a[9 * i + line], narrow_b[9 * i + line]
            low, high = jnp.where(odd_n, a, b), jnp.where(odd_n, b, a)

            def spread(row):
                return jnp.where(
                    first_column,
                    jnp.where(lowest, low[row : row + 1], high[row : row + 1]),
                    jnp.where(lowest, low[row + 1 : row + 2], high[row + 1 : row + 2]),
                )

            other.append(jnp.where(wall, image[i], jnp.where(top, near[i], spread(0))))
            edge = jnp.logical_or(wall, top)
            other_slope.append(jnp.where(edge, slope[i], spread(2)))
        return other, other_slope

    outer(nodes, rate, 0, first_column, sub >= 0, across)
    outer(nodes, rate, 1, lowest, jnp.logical_or(lowest, height == 3), upright)

    @pl.when(at_bottom)
    def _():
        def strip_vector(k):
            left, right = sides(k)
            tile, row = (COLUMN + k, 0) if k < HALF else (COLUMN + k - HALF, 2)
            far_left, far_right = sides(tile)
            return jnp.concatenate(
                [far_left[row : row + 2], left[0:2], right[0:2], far_right[row : row + 2]], axis=0
            )

        fill(strip_vector, strip_nodes, strip_pre)
        interior(strip_nodes, strip_pre, strip_rate, 2)
        strip_lower = lax.rem(sub, 4) < 2

        def own(i, node):
            x = nodes[i, node]
            return jnp.where(first_column, roll(x, 2), x)

        def towards_brick(line, near, slope):
            at = nodes_of(line, 0)
            u = [[own(i, m) for i in range(5)] for m in at]
            near = [jnp.where(strip_lower, c, a) for a, c in zip(u[0], u[2])]
            away = [jnp.where(strip_lower, a, c) for a, c in zip(u[0], u[2])]
            other = [edge_slope(*x) for x in zip(near, u[1], away)]
            return near, [jnp.where(strip_lower, x, -x) for x in other]

        middle = jnp.logical_and(sub >= 2, sub < 6)
        outer(strip_nodes, strip_rate, 0, strip_lower, middle, towards_brick)
        strip_lowest = lax.rem(sub, 2) == 0

        def above(k):
            x = both_sides(k, k)
            return jnp.where(first_column, roll(x, 1), roll(x, -1))

        def strip_upright(line, near, slope):
            at = nodes_of(line, 1)
            u = [[above(27 * i + m) for i in range(5)] for m in at]
            other = [-edge_slope(*x) for x in zip(*u)]
            image = mirrored(near)
            return (
                [jnp.where(strip_lowest, x, y) for x, y in zip(image, u[0])],
                [jnp.where(strip_lowest, x, y) for x, y in zip(slope, other)],
            )

        outer(strip_nodes, strip_rate, 1, strip_lowest, sub >= 0, strip_upright)

        left, right = sides(WIDE_TILES - 1)

        def in_row(row):
            parts = [left[row + 2 : row + 3]] * 2 + [left[row : row + 1]]
            parts += [tables[row : row + 1], tables[row + 2 : row + 3]]
            parts += [right[row : row + 1]] + [right[row + 2 : row + 3]] * 2
            return jnp.concatenate(parts, axis=0)

        code = in_row(0)
        codes[...] = code
        factorize(code, in_row(1), fractions, taken, scaled, factor)


def cut_solve(code, rate, strip_rate, scaled, factor):
    sub = sublane()
    is_cut = code > 0.0
    masks = masks_of(code)
    has_target = source_of(masks[0], 0) + masks[1] + source_of(masks[2], 2) > 0.0

    def in_row(i, n):
        s, m = strip_rate[i, n], rate[i, n]
        s = jnp.where(lax.rem(sub, 2) == 1, roll(s, 1), s)
        return jnp.where(sub == 3, roll(m, 3), jnp.where(sub == 4, m, s))

    def in_second_row(i, n):
        s, m = strip_rate[i, n], rate[i, n]
        s = jnp.where(sub == 2, roll(s, -1), s)
        return jnp.where(sub == 3, roll(m, 2), jnp.where(sub == 4, roll(m, -1), s))

    def solve(i, carry):
        for c in range(3):
            y = []
            for a in range(3):
                at = [9 * a + 3 * b + c for b in range(3)]
                y.append(below_columns([scaled[n] * in_row(i, n) for n in at]))
            x = [None] * 9
            for b in range(3):
                line = [y[a][b] for a in range(3)]
                parts = (above_columns(line), line, below_columns(line))
                for a in range(3):
                    total = weight(a, b, c) * in_second_row(i, 9 * a + 3 * b + c)
                    for k in range(3):
                        total += source_of(jnp.where(masks[k] > 0.0, parts[k][a], 0.0), k)
                    x[3 * a + b] = total
            for m, (r, j) in enumerate(BELOW_DIAGONAL):
                x[r] = x[r] - factor[c, m] * x[j]
            x = [x[j] * factor[c, 36 + j] for j in range(9)]
            for m, (r, j) in reversed(tuple(enumerate(BELOW_DIAGONAL))):
                x[j] = x[j] - factor[c, m] * x[r]
            y = []
            for a in range(3):
                line = [
                    jnp.where(masks[0] > 0.0, roll(s, 1), jnp.where(masks[2] > 0.0, roll(s, -1), s))
                    for s in x[3 * a : 3 * a + 3]
                ]
                y.append(below_rows(line))
            for b in range(3):
                line = [y[a][b] for a in range(3)]
                one, three = above_rows(line), below_rows(line)
                for a in range(3):
                    n = 9 * a + 3 * b + c
                    update = jnp.where(masks[0] > 0.0, one[a], jnp.where(masks[2] > 0.0, three[a], line[a]))
                    target = x[3 * a + b]
                    m = rate[i, n]
                    m = jnp.where(cut_low, roll(update, -3), jnp.where(cut_high, update, m))
                    m = jnp.where(target_low, roll(target, -2), m)
                    rate[i, n] = jnp.where(target_high, roll(target, 1), m)
        return carry

    cut, taking = is_cut.astype(jnp.float32), has_target.astype(jnp.float32)
    cut_low = jnp.logical_and(sub == 0, roll(cut, -3) > 0.0)
    cut_high = jnp.logical_and(sub == 4, is_cut)
    target_low = jnp.logical_and(sub == 1, roll(taking, -2) > 0.0)
    target_high = jnp.logical_and(sub == 5, roll(taking, 1) > 0.0)
    lax.fori_loop(0, 5, solve, 0)


def last_kernel(
    start,
    nodes,
    rate_in,
    strip_nodes,
    strip_rate_in,
    codes,
    scaled,
    factor,
    narrow_b,
    far,
    out,
    rate,
    strip_rate,
):
    rate[...] = rate_in[...]
    low_pair = lax.rem(lax.axis_index("wide"), 4) < 2
    sub = sublane()

    @pl.when(lax.axis_index("narrow") == 0)
    def _():
        strip_rate[...] = strip_rate_in[...]
        left_side = sub < 4
        use_far = jnp.logical_xor(left_side, jnp.logical_not(low_pair))

        def beyond(line, near, slope):
            def value(i, row):
                m = 9 * i + line
                return jnp.where(use_far, far[m, row : row + 1, :], narrow_b[m, row : row + 1, :])

            return [value(i, 0) for i in range(5)], [value(i, 2) for i in range(5)]

        ends = jnp.logical_or(sub == 0, sub == 6)
        outer(strip_nodes, strip_rate, 0, lax.rem(sub, 4) < 2, ends, beyond)
        cut_solve(codes[...], rate, strip_rate, scaled, factor)

    for k in range(COLUMN):
        i, n = divmod(k, NODES)
        value = 0.25 * nodes[i, n] + 0.0075 * rate[i, n]
        out[k] = 0.75 * start[k] + value[0:4]
        out[COLUMN + k] = 0.75 * start[COLUMN + k] + value[4:8]


def as_tiles(x):
    return jnp.transpose(x, (0, 2, 3, 1, 4)).reshape(2 * COLUMN, 4, 128)


def from_tiles(x):
    return jnp.transpose(x.reshape(2, 5, NODES, 4, 128), (0, 3, 1, 2, 4))


def device_step(wide, narrow, section_start, section_state, cut_code, cut_rule, rule_fractions):
    f32 = jnp.float32

    def call(kernel, name, shapes, operands, scratch=(), flops=0):
        vmem = pl.BlockSpec(memory_space=pltpu.VMEM)
        cost = pl.CostEstimate(flops=flops, bytes_accessed=0, transcendentals=0) if flops else None
        return pl.pallas_call(
            kernel,
            name=name,
            out_shape=[jax.ShapeDtypeStruct(s, f32) for s in shapes],
            in_specs=[vmem] * len(operands),
            out_specs=[vmem] * len(shapes),
            scratch_shapes=list(scratch),
            cost_estimate=cost,
            compiler_params=pltpu.CompilerParams(vmem_limit_bytes=8 * 2**20),
        )(*operands)

    state, start = as_tiles(section_state), as_tiles(section_start)
    wide_shape, narrow_shape = (WIDE_TILES, 4, 128), (NARROW_TILES, 4, 128)
    tables = jnp.stack([cut_code, cut_rule], axis=1).reshape(4, 128).astype(f32)
    mine_a, mine_b = call(pack_wide, "pack_wide", [wide_shape] * 2, (state, tables))
    far, up_a, up_b = call(
        pack_rest, "pack_rest", [(FAR_TILES, 4, 128), narrow_shape, narrow_shape], (state,)
    )

    both = ("wide", "narrow")
    cross = swaps([(2 * j + 1, (2 * j + 2) % wide) for j in range(wide // 2)])
    inside = swaps([(2 * j, 2 * j + 1) for j in range(wide // 2)])
    even = swaps([(2 * j, 2 * j + 1) for j in range(narrow // 2)])
    between = [(2 * j + 1, 2 * j + 2) for j in range(narrow // 2 - 1)]
    far_inside = [(4 * j + k, 4 * j + 2 + k) for j in range(wide // 4) for k in (0, 1)]
    far_cross = [(4 * j + 2 + k, (4 * j + 4 + k) % wide) for j in range(wide // 4) for k in (0, 1)]
    mixed = [(narrow * i + a, narrow * i + b) for i in range(wide) for a, b in between]
    mixed = swaps(mixed + [(narrow * a, narrow * b) for a, b in far_inside])
    far_cross = swaps([(narrow * a, narrow * b) for a, b in far_cross])

    wide_a = lax.ppermute(mine_a, "wide", cross)
    wide_b = lax.ppermute(mine_b, "wide", inside)
    far = lax.ppermute(far, both, far_cross)
    narrow_a = lax.ppermute(up_a, "narrow", even)
    narrow_b = lax.ppermute(up_b, both, mixed)

    full = (5, NODES, 8, 128)
    thermal = pltpu.VMEM((3, NODES, 8, 128), f32)
    nodes, rate = call(inner_kernel, "inner", [full, full], (state,), [thermal], flops=10**9)
    rate, strip_nodes, strip_rate, codes, scaled, factor = call(
        edge_kernel,
        "edge",
        [full, full, full, (8, 128), (NODES, 8, 128), (3, 45, 8, 128)],
        (nodes, rate, wide_a, wide_b, narrow_a, narrow_b, tables, rule_fractions.T),
        scratch=[pltpu.VMEM((8 * 32, 128), f32), thermal],
        flops=10**9,
    )
    (out,) = call(
        last_kernel,
        "last",
        [(2 * COLUMN, 4, 128)],
        (start, nodes, rate, strip_nodes, strip_rate, codes, scaled, factor, narrow_b, far),
        scratch=[pltpu.VMEM(full, f32)] * 2,
    )
    return from_tiles(out)


def solution(mesh):
    return jax.shard_map(
        functools.partial(device_step, mesh.shape["wide"], mesh.shape["narrow"]),
        mesh=mesh,
        in_specs=(
            P("wide", "narrow", None, None, None),
            P("wide", "narrow", None, None, None),
            P("wide", None),
            P("wide", None),
            P(),
        ),
        out_specs=P("wide", "narrow", None, None, None),
        check_vma=False,
    )
```

```python
import functools

import jax
import jax.numpy as jnp
from jax import lax
from jax.experimental import pallas as pl
from jax.experimental.pallas import tpu as pltpu
from jax.sharding import PartitionSpec as P

NODES = 27
COLUMN = 5 * NODES
HALF = 68
WIDE_TILES = COLUMN + HALF + 1
NARROW_TILES = 45


def swaps(pairs):
    return [p for a, b in pairs for p in ((a, b), (b, a))]


def nodes_of(line, d):
    base = (line, 9 * (line // 3) + line % 3, 3 * line)[d]
    return [base + (9, 3, 1)[d] * k for k in range(3)]


def sublane():
    return lax.broadcasted_iota(jnp.int32, (8, 128), 0)


def roll(x, shift):
    return pltpu.roll(x, shift % 8, 0)


def edge_slope(near, middle, away):
    return 1.5 * near - 2.0 * middle + 0.5 * away


def edge_of(state, column, i, line, d, high):
    at = [27 * i + k for k in nodes_of(line, d)]
    if column is None:
        u = [jnp.concatenate([state[k], state[COLUMN + k]], axis=0) for k in at]
    else:
        u = [state[column * COLUMN + k] for k in at]
    near, away = jnp.where(high, u[2], u[0]), jnp.where(high, u[0], u[2])
    slope = edge_slope(near, u[1], away)
    return near, jnp.where(high, slope, -slope)


def put_upright(state, target, high):
    for i in range(5):
        for line in range(9):
            near, slope = edge_of(state, None, i, line, 1, high)
            for row, x in ((0, near), (2, slope)):
                target[9 * i + line, row : row + 1, :] = jnp.where(high, x[3:4], x[0:1])
                target[9 * i + line, row + 1 : row + 2, :] = jnp.where(high, x[7:8], x[4:5])


def pack_wide(state, tables, wide_a, wide_b):
    odd, n = lax.rem(lax.axis_index("wide"), 2), lax.axis_index("narrow")

    @pl.when(n == 0)
    def _():
        for target, near in ((wide_a, odd), (wide_b, 1 - odd)):
            first, other = near * COLUMN, (1 - near) * COLUMN
            target[0:COLUMN] = state[pl.ds(first, COLUMN)]
            for m in range(HALF):
                later = min(m + HALF, COLUMN - 1)
                target[COLUMN + m, 0:2, :] = state[other + m, 0:2, :]
                target[COLUMN + m, 2:4, :] = state[other + later, 0:2, :]
            own, swapped = tables[...], jnp.concatenate([tables[2:4], tables[0:2]], axis=0)
            target[WIDE_TILES - 1] = jnp.where(near == 0, own, swapped)

    @pl.when(n > 0)
    def _():
        put_upright(state, wide_b, lax.rem(n, 2) == 1)
        for i in range(5):
            for line in range(9):
                near, slope = edge_of(state, 1 - odd, i, line, 0, odd == 0)
                wide_a[9 * i + line], wide_a[NARROW_TILES + 9 * i + line] = near, slope


def pack_rest(state, narrow, far_a, far_b):
    w, n = lax.axis_index("wide"), lax.axis_index("narrow")
    odd, low_pair = lax.rem(w, 2), (lax.rem(w, 4) < 2).astype(jnp.int32)
    put_upright(state, narrow, lax.rem(n, 2) == 0)

    @pl.when(n == 0)
    def _():
        for target, column in ((far_a, 1 - low_pair), (far_b, low_pair)):
            for i in range(5):
                for line in range(9):
                    for k, x in zip((0, 45), edge_of(state, column, i, line, 0, column == 1)):
                        m = k + 9 * i + line
                        target[m // 4, m % 4 : m % 4 + 1, :] = x[0:1]

    @pl.when(n > 0)
    def _():
        for i in range(5):
            for line in range(9):
                m = 9 * i + line
                far_a[m], far_b[m] = edge_of(state, odd, i, line, 0, odd == 1)


def pressure_of(v, inverse):
    return 0.4 * (v[4] - 0.5 * (v[1] * v[1] + v[2] * v[2] + v[3] * v[3]) * inverse)


def flux(v, d, inverse, pressure, sound):
    speed = v[1 + d] * inverse
    out = [v[1 + d], v[1] * speed, v[2] * speed, v[3] * speed, (v[4] + pressure) * speed]
    out[1 + d] = out[1 + d] + pressure
    return out, jnp.abs(speed) + sound


def thermo(v):
    inverse = 1.0 / v[0]
    pressure = pressure_of(v, inverse)
    return inverse, pressure, jnp.sqrt(1.4 * pressure * inverse)


def load(ref, node):
    return [ref[i, node] for i in range(5)]


def fill(vector, nodes, pre):
    for n in range(NODES):
        v = [vector(27 * i + n) for i in range(5)]
        for i in range(5):
            nodes[i, n] = v[i]
        for j, x in enumerate(thermo(v)):
            pre[j, n] = x


def interior(nodes, pre, rate, height):
    sub = sublane()
    inner_x = lax.rem(sub, 2 * height) >= height
    inner_y = lax.rem(sub, height) > 0
    moves = (
        (lambda x: roll(x, height), lambda x: roll(x, -height), inner_x),
        (lambda x: roll(x, 1), lambda x: roll(x, -1), inner_y),
        (lambda x: pltpu.roll(x, 1, 1), lambda x: pltpu.roll(x, 127, 1), None),
    )
    for d in range(3):
        ahead, back, inner = moves[d]

        def body(line, carry, d=d, ahead=ahead, back=back, inner=inner):
            base = (line, 9 * (line // 3) + lax.rem(line, 3), 3 * line)[d]
            at = [base + (9, 3, 1)[d] * k for k in range(3)]
            v = [load(nodes, n) for n in at]
            f, speeds = zip(*[flux(v[k], d, *[pre[j, at[k]] for j in range(3)]) for k in range(3)])
            speed = 0.5 * jnp.maximum(speeds[0], ahead(speeds[2]))
            for i in range(5):
                a, b, c = v[0][i], v[1][i], v[2][i]
                g_low = f[0][i] + 0.1 * edge_slope(a, b, c)
                g_mid = f[1][i] - 0.05 * (c - a)
                g_high = f[2][i] - 0.1 * edge_slope(c, b, a)
                jump = a - ahead(c)
                lift = 0.075 * jump
                face = 1.5 * (ahead(g_high) + g_low) - 3.0 * (speed * jump) - 3.0 * lift
                if inner is not None:
                    face, lift = jnp.where(inner, face, 0.0), jnp.where(inner, lift, 0.0)
                face_up, lift_up = back(face), back(lift)
                first = face - lift_up - 1.5 * g_low - 2.0 * g_mid + 0.5 * g_high
                second = lift_up - lift + 0.5 * (g_low - g_high)
                third = lift - face_up - 0.5 * g_low + 2.0 * g_mid + 1.5 * g_high
                for n, x in zip(at, (first, second, third)):
                    rate[i, n] = x if d == 0 else rate[i, n] + x
            return carry

        lax.fori_loop(0, 9, body, 0)


def outer(nodes, rate, d, lower, active, halo):
    turn = jnp.where(lower, 1.0, -1.0)
    for line in range(9):
        at = nodes_of(line, d)
        v = [load(nodes, n) for n in at]
        near = [jnp.where(lower, a, c) for a, c in zip(v[0], v[2])]
        away = [jnp.where(lower, c, a) for a, c in zip(v[0], v[2])]
        slope = [-turn * edge_slope(*x) for x in zip(near, v[1], away)]
        other, other_slope = halo(line, near, slope)
        f, speed = flux(near, d, *thermo(near))
        f_other, speed_other = flux(other, d, *thermo(other))
        half = 0.5 * jnp.maximum(speed, speed_other)
        for i in range(5):
            jump = turn * (near[i] - other[i])
            face = (
                0.5 * (f[i] + f_other[i])
                - half * jump
                - 0.05 * (slope[i] + other_slope[i])
                - 0.15 * jump
            )
            edge = jnp.where(active, turn * (3.0 * face + 0.225 * jump), 0.0)
            lift = jnp.where(active, turn * (0.075 * jump), 0.0)
            rate[i, at[0]] += jnp.where(lower, edge, lift)
            rate[i, at[1]] -= lift
            rate[i, at[2]] += jnp.where(lower, lift, edge)


def mirrored(v):
    return [v[0], -v[1], -v[2], -v[3], v[4]]


def inner_kernel(state, nodes, rate, pre):
    fill(lambda k: jnp.concatenate([state[k], state[COLUMN + k]], axis=0), nodes, pre)
    interior(nodes, pre, rate, 4)


def below_rows(x):
    return [6.0 * x[0] - 8.0 * x[1] + 3.0 * x[2], 3.0 * x[0] - 3.0 * x[1] + x[2], x[0]]


def above_rows(x):
    return [x[2], x[0] - 3.0 * x[1] + 3.0 * x[2], 3.0 * x[0] - 8.0 * x[1] + 6.0 * x[2]]


def below_columns(x):
    return [6.0 * x[0] + 3.0 * x[1] + x[2], -8.0 * x[0] - 3.0 * x[1], 3.0 * x[0] + x[1]]


def above_columns(x):
    return [x[1] + 3.0 * x[2], -3.0 * x[1] - 8.0 * x[2], x[0] + 3.0 * x[1] + 6.0 * x[2]]


BELOW = ((6.0, -8.0, 3.0), (3.0, -3.0, 1.0), (1.0, 0.0, 0.0))
ABOVE = ((0.0, 0.0, 1.0), (1.0, -3.0, 3.0), (3.0, -8.0, 6.0))
ENDS = (1.0 / 3.0, 4.0 / 3.0, 1.0 / 3.0)
PAIRS = tuple((i, j) for i in range(3) for j in range(i + 1))
BELOW_DIAGONAL = tuple((r, j) for j in range(9) for r in range(j + 1, 9))


def weight(a, b, c):
    return ENDS[a] * ENDS[b] * ENDS[c]


def combine(table, x, i, j):
    total = None
    for k in range(3):
        factor = table[k][i] * table[k][j]
        if factor != 0.0:
            term = x[k] if factor == 1.0 else factor * x[k]
            total = term if total is None else total + term
    return total


def source_of(x, k):
    return (roll(x, -1), x, roll(x, 1))[k]


def masks_of(code):
    return [(code == float(k)).astype(jnp.float32) for k in (1, 2, 3)]


def factorize(code, rule, fractions, taken, scaled, factor):
    index = lax.broadcasted_iota(jnp.int32, (64, 128), 0).astype(jnp.float32)
    onehot = jnp.concatenate(
        [(index == rule[j : j + 1, :]).astype(jnp.float32) for j in range(8)], axis=1
    )
    shares = lax.dot_general(
        fractions[...],
        onehot,
        (((1,), (0,)), ((), ())),
        precision=lax.Precision.HIGHEST,
        preferred_element_type=jnp.float32,
    )
    for j in range(8):
        taken[32 * j : 32 * j + 27, :] = shares[:, 128 * j : 128 * j + 128]
    is_cut = code > 0.0
    masks = masks_of(code)
    for c in range(3):
        inner = [[None] * 3 for _ in range(3)]
        for a in range(3):
            parts = [[], [], []]
            for b in range(3):
                n = 9 * a + 3 * b + c
                amount = jnp.where(is_cut, weight(a, b, c) * taken[pl.ds(n, 8, stride=32), :], 0.0)
                scaled[n] = amount
                for k in range(3):
                    parts[k].append(source_of(jnp.where(masks[k] > 0.0, amount, 0.0), k))
            for k in range(3):
                inner[k][a] = {p: combine(BELOW, parts[k], *p) for p in PAIRS}
        matrix = {}
        for row in range(9):
            for column in range(row + 1):
                (a, b), (a2, b2) = divmod(row, 3), divmod(column, 3)
                p = (max(b, b2), min(b, b2))
                total = combine(ABOVE, [inner[0][i][p] for i in range(3)], a, a2)
                third = combine(BELOW, [inner[2][i][p] for i in range(3)], a, a2)
                if third is not None:
                    total = third if total is None else total + third
                if a == a2:
                    total = total + inner[1][a][p]
                if row == column:
                    total = total + weight(a, b, c)
                matrix[row, column] = total
        for j in range(9):
            inverse = 1.0 / matrix[j, j]
            factor[c, 36 + j] = inverse
            lower = {r: matrix[r, j] * inverse for r in range(j + 1, 9)}
            for r in range(j + 1, 9):
                factor[c, BELOW_DIAGONAL.index((r, j))] = lower[r]
                for s in range(j + 1, r + 1):
                    matrix[r, s] = matrix[r, s] - lower[r] * matrix[s, j]


def edge_kernel(
    nodes,
    rate_in,
    wide_a,
    wide_b,
    narrow,
    tables,
    fractions,
    rate,
    strip_nodes,
    strip_rate,
    codes,
    scaled,
    factor,
    taken,
    strip_pre,
):
    rate[...] = rate_in[...]
    w, n = lax.axis_index("wide"), lax.axis_index("narrow")
    odd = lax.rem(w, 2) == 1
    odd_n, at_bottom, at_top = lax.rem(n, 2) == 1, n == 0, n == lax.axis_size("narrow") - 1
    sub = sublane()
    first_column = sub < 4
    height = lax.rem(sub, 4)

    def sides(k):
        a, b = wide_a[k], wide_b[k]
        return jnp.where(odd, b, a), jnp.where(odd, a, b)

    def both_sides(k_left, k_right):
        return jnp.concatenate([sides(k_left)[0], sides(k_right)[1]], axis=0)

    def across(line, near, slope):
        at = nodes_of(line, 0)
        u = [
            [both_sides(27 * i + at[2 - j], 27 * i + at[j]) for i in range(5)] for j in range(3)
        ]
        other = [edge_slope(*x) for x in zip(*u)]
        return u[0], [jnp.where(first_column, x, -x) for x in other]

    lowest = height == 0
    wall = jnp.logical_and(lowest, at_bottom)
    top = jnp.logical_and(height == 3, at_top)

    def upright(line, near, slope):
        other, other_slope = [], []
        image = mirrored(near)
        for i in range(5):
            a, b = narrow[9 * i + line], wide_b[9 * i + line]
            low, high = jnp.where(odd_n, a, b), jnp.where(odd_n, b, a)

            def spread(row):
                return jnp.where(
                    first_column,
                    jnp.where(lowest, low[row : row + 1], high[row : row + 1]),
                    jnp.where(lowest, low[row + 1 : row + 2], high[row + 1 : row + 2]),
                )

            other.append(jnp.where(wall, image[i], jnp.where(top, near[i], spread(0))))
            edge = jnp.logical_or(wall, top)
            other_slope.append(jnp.where(edge, slope[i], spread(2)))
        return other, other_slope

    outer(nodes, rate, 1, lowest, jnp.logical_or(lowest, height == 3), upright)

    @pl.when(at_bottom)
    def _():
        outer(nodes, rate, 0, first_column, sub >= 0, across)

        def strip_vector(k):
            left, right = sides(k)
            tile, row = (COLUMN + k, 0) if k < HALF else (COLUMN + k - HALF, 2)
            far_left, far_right = sides(tile)
            return jnp.concatenate(
                [far_left[row : row + 2], left[0:2], right[0:2], far_right[row : row + 2]], axis=0
            )

        fill(strip_vector, strip_nodes, strip_pre)
        interior(strip_nodes, strip_pre, strip_rate, 2)
        strip_lower = lax.rem(sub, 4) < 2

        def own(i, node):
            x = nodes[i, node]
            return jnp.where(first_column, roll(x, 2), x)

        def towards_brick(line, near, slope):
            at = nodes_of(line, 0)
            u = [[own(i, m) for i in range(5)] for m in at]
            near = [jnp.where(strip_lower, c, a) for a, c in zip(u[0], u[2])]
            away = [jnp.where(strip_lower, a, c) for a, c in zip(u[0], u[2])]
            other = [edge_slope(*x) for x in zip(near, u[1], away)]
            return near, [jnp.where(strip_lower, x, -x) for x in other]

        middle = jnp.logical_and(sub >= 2, sub < 6)
        outer(strip_nodes, strip_rate, 0, strip_lower, middle, towards_brick)
        strip_lowest = lax.rem(sub, 2) == 0

        def above(k):
            x = both_sides(k, k)
            return jnp.where(first_column, roll(x, 1), roll(x, -1))

        def strip_upright(line, near, slope):
            at = nodes_of(line, 1)
            u = [[above(27 * i + m) for i in range(5)] for m in at]
            other = [-edge_slope(*x) for x in zip(*u)]
            image = mirrored(near)
            return (
                [jnp.where(strip_lowest, x, y) for x, y in zip(image, u[0])],
                [jnp.where(strip_lowest, x, y) for x, y in zip(slope, other)],
            )

        outer(strip_nodes, strip_rate, 1, strip_lowest, sub >= 0, strip_upright)

        left, right = sides(WIDE_TILES - 1)

        def in_row(row):
            parts = [left[row + 2 : row + 3]] * 2 + [left[row : row + 1]]
            parts += [tables[row : row + 1], tables[row + 2 : row + 3]]
            parts += [right[row : row + 1]] + [right[row + 2 : row + 3]] * 2
            return jnp.concatenate(parts, axis=0)

        code = in_row(0)
        codes[...] = code
        factorize(code, in_row(1), fractions, taken, scaled, factor)


def cut_solve(code, rate, strip_rate, scaled, factor):
    sub = sublane()
    is_cut = code > 0.0
    masks = masks_of(code)
    has_target = source_of(masks[0], 0) + masks[1] + source_of(masks[2], 2) > 0.0

    def in_row(i, n):
        s, m = strip_rate[i, n], rate[i, n]
        s = jnp.where(lax.rem(sub, 2) == 1, roll(s, 1), s)
        return jnp.where(sub == 3, roll(m, 3), jnp.where(sub == 4, m, s))

    def in_second_row(i, n):
        s, m = strip_rate[i, n], rate[i, n]
        s = jnp.where(sub == 2, roll(s, -1), s)
        return jnp.where(sub == 3, roll(m, 2), jnp.where(sub == 4, roll(m, -1), s))

    def solve(i, carry):
        for c in range(3):
            y = []
            for a in range(3):
                at = [9 * a + 3 * b + c for b in range(3)]
                y.append(below_columns([scaled[n] * in_row(i, n) for n in at]))
            x = [None] * 9
            for b in range(3):
                line = [y[a][b] for a in range(3)]
                parts = (above_columns(line), line, below_columns(line))
                for a in range(3):
                    total = weight(a, b, c) * in_second_row(i, 9 * a + 3 * b + c)
                    for k in range(3):
                        total += source_of(jnp.where(masks[k] > 0.0, parts[k][a], 0.0), k)
                    x[3 * a + b] = total
            for m, (r, j) in enumerate(BELOW_DIAGONAL):
                x[r] = x[r] - factor[c, m] * x[j]
            x = [x[j] * factor[c, 36 + j] for j in range(9)]
            for m, (r, j) in reversed(tuple(enumerate(BELOW_DIAGONAL))):
                x[j] = x[j] - factor[c, m] * x[r]
            y = []
            for a in range(3):
                line = [
                    jnp.where(masks[0] > 0.0, roll(s, 1), jnp.where(masks[2] > 0.0, roll(s, -1), s))
                    for s in x[3 * a : 3 * a + 3]
                ]
                y.append(below_rows(line))
            for b in range(3):
                line = [y[a][b] for a in range(3)]
                one, three = above_rows(line), below_rows(line)
                for a in range(3):
                    n = 9 * a + 3 * b + c
                    update = jnp.where(masks[0] > 0.0, one[a], jnp.where(masks[2] > 0.0, three[a], line[a]))
                    target = x[3 * a + b]
                    m = rate[i, n]
                    m = jnp.where(cut_low, roll(update, -3), jnp.where(cut_high, update, m))
                    m = jnp.where(target_low, roll(target, -2), m)
                    rate[i, n] = jnp.where(target_high, roll(target, 1), m)
        return carry

    cut, taking = is_cut.astype(jnp.float32), has_target.astype(jnp.float32)
    cut_low = jnp.logical_and(sub == 0, roll(cut, -3) > 0.0)
    cut_high = jnp.logical_and(sub == 4, is_cut)
    target_low = jnp.logical_and(sub == 1, roll(taking, -2) > 0.0)
    target_high = jnp.logical_and(sub == 5, roll(taking, 1) > 0.0)
    lax.fori_loop(0, 5, solve, 0)


def last_kernel(
    start,
    nodes,
    rate_in,
    strip_nodes,
    strip_rate,
    codes,
    scaled,
    factor,
    wide_a,
    far_a,
    far_b,
    out,
    rate,
    ends_rate,
):
    rate[...] = rate_in[...]
    w, n = lax.axis_index("wide"), lax.axis_index("narrow")
    odd, low_pair = lax.rem(w, 2) == 1, lax.rem(w, 4) < 2
    sub = sublane()
    first_column = sub < 4

    @pl.when(n == 0)
    def _():
        ends_rate[...] = strip_rate[...]
        use_far = jnp.logical_xor(first_column, jnp.logical_not(low_pair))

        def value(m):
            tile, row = m // 4, pl.ds(m % 4, 1)
            return jnp.where(use_far, far_a[tile, row, :], far_b[tile, row, :])

        def beyond(line, near, slope):
            at = [9 * i + line for i in range(5)]
            return [value(m) for m in at], [value(45 + m) for m in at]

        ends = jnp.logical_or(sub == 0, sub == 6)
        outer(strip_nodes, ends_rate, 0, lax.rem(sub, 4) < 2, ends, beyond)
        cut_solve(codes[...], rate, ends_rate, scaled, factor)

    def across(line, near, slope):
        def value(a, b):
            return jnp.concatenate([jnp.where(odd, b, a), jnp.where(odd, a, b)], axis=0)

        at = [9 * i + line for i in range(5)]
        return (
            [value(far_a[m], wide_a[m]) for m in at],
            [value(far_b[m], wide_a[NARROW_TILES + m]) for m in at],
        )

    @pl.when(n > 0)
    def _():
        outer(nodes, rate, 0, first_column, sub >= 0, across)

    for k in range(COLUMN):
        i, n = divmod(k, NODES)
        value = 0.25 * nodes[i, n] + 0.0075 * rate[i, n]
        out[k] = 0.75 * start[k] + value[0:4]
        out[COLUMN + k] = 0.75 * start[COLUMN + k] + value[4:8]


def as_tiles(x):
    return jnp.transpose(x, (0, 2, 3, 1, 4)).reshape(2 * COLUMN, 4, 128)


def from_tiles(x):
    return jnp.transpose(x.reshape(2, 5, NODES, 4, 128), (0, 3, 1, 2, 4))


def device_step(wide, narrow, section_start, section_state, cut_code, cut_rule, rule_fractions):
    f32 = jnp.float32

    def call(kernel, name, shapes, operands, scratch=(), flops=0):
        vmem = pl.BlockSpec(memory_space=pltpu.VMEM)
        cost = pl.CostEstimate(flops=flops, bytes_accessed=0, transcendentals=0) if flops else None
        return pl.pallas_call(
            kernel,
            name=name,
            out_shape=[jax.ShapeDtypeStruct(s, f32) for s in shapes],
            in_specs=[vmem] * len(operands),
            out_specs=[vmem] * len(shapes),
            scratch_shapes=list(scratch),
            cost_estimate=cost,
            compiler_params=pltpu.CompilerParams(vmem_limit_bytes=8 * 2**20),
        )(*operands)

    state, start = as_tiles(section_state), as_tiles(section_start)
    wide_shape, narrow_shape = (WIDE_TILES, 4, 128), (NARROW_TILES, 4, 128)
    tables = jnp.stack([cut_code, cut_rule], axis=1).reshape(4, 128).astype(f32)
    mine_a, mine_b = call(pack_wide, "pack_wide", [wide_shape] * 2, (state, tables))
    up, far_a, far_b = call(pack_rest, "pack_rest", [narrow_shape] * 3, (state,))

    both = ("wide", "narrow")
    half = wide // 2
    cross = swaps([(2 * j + 1, (2 * j + 2) % wide) for j in range(half)])
    inside = swaps([(2 * j, 2 * j + 1) for j in range(half)])
    far_inside = swaps([(4 * j + k, 4 * j + 2 + k) for j in range(wide // 4) for k in (0, 1)])
    far_cross = [(4 * j + 2 + k, (4 * j + 4 + k) % wide) for j in range(wide // 4) for k in (0, 1)]
    far_cross = swaps(far_cross)
    even = swaps([(2 * j, 2 * j + 1) for j in range(narrow // 2)])
    between = swaps([(2 * j + 1, 2 * j + 2) for j in range(narrow // 2 - 1)])
    unused = swaps([(16 * j + k, 16 * j + 8 + k) for j in range(wide // 16) for k in range(8)])

    def along_wide(pairs, *rows):
        return [(narrow * a + n, narrow * b + n) for a, b in pairs for n in rows]

    def along_narrow(pairs):
        return [(narrow * w + a, narrow * w + b) for w in range(wide) for a, b in pairs]

    others = range(1, narrow)
    wide_a = lax.ppermute(mine_a, both, along_wide(cross, 0) + along_wide(inside, *others))
    wide_b = lax.ppermute(
        mine_b,
        both,
        along_wide(inside, 0) + along_narrow(between) + along_wide(unused, narrow - 1),
    )
    narrow_got = lax.ppermute(up, both, along_narrow(even))
    far_a = lax.ppermute(far_a, both, along_wide(far_cross, 0) + along_wide(cross, *others))
    far_b = lax.ppermute(far_b, both, along_wide(far_inside, 0) + along_wide(cross, *others))

    full = (5, NODES, 8, 128)
    thermal = pltpu.VMEM((3, NODES, 8, 128), f32)
    nodes, rate = call(inner_kernel, "inner", [full, full], (state,), [thermal], flops=10**9)
    rate, *strip = call(
        edge_kernel,
        "edge",
        [full, full, full, (8, 128), (NODES, 8, 128), (3, 45, 8, 128)],
        (nodes, rate, wide_a, wide_b, narrow_got, tables, rule_fractions.T),
        scratch=[pltpu.VMEM((8 * 32, 128), f32), thermal],
        flops=10**9,
    )
    (out,) = call(
        last_kernel,
        "last",
        [(2 * COLUMN, 4, 128)],
        (start, nodes, rate, *strip, wide_a, far_a, far_b),
        scratch=[pltpu.VMEM(full, f32)] * 2,
    )
    return from_tiles(out)


def solution(mesh):
    return jax.shard_map(
        functools.partial(device_step, mesh.shape["wide"], mesh.shape["narrow"]),
        mesh=mesh,
        in_specs=(
            P("wide", "narrow", None, None, None),
            P("wide", "narrow", None, None, None),
            P("wide", None),
            P("wide", None),
            P(),
        ),
        out_specs=P("wide", "narrow", None, None, None),
        check_vma=False,
    )
```

```python
import functools

import jax
import jax.numpy as jnp
from jax import lax
from jax.experimental import pallas as pl
from jax.experimental.pallas import tpu as pltpu
from jax.sharding import PartitionSpec as P

NODES = 27
COLUMN = 5 * NODES
HALF = 68
WIDE_TILES = COLUMN + HALF + 1
NARROW_TILES = 45


def swaps(pairs):
    return [p for a, b in pairs for p in ((a, b), (b, a))]


def nodes_of(line, d):
    base = (line, 9 * (line // 3) + line % 3, 3 * line)[d]
    return [base + (9, 3, 1)[d] * k for k in range(3)]


def sublane():
    return lax.broadcasted_iota(jnp.int32, (8, 128), 0)


def roll(x, shift):
    return pltpu.roll(x, shift % 8, 0)


def edge_slope(near, middle, away):
    return 1.5 * near - 2.0 * middle + 0.5 * away


def edge_of(state, column, i, line, d, high):
    at = [27 * i + k for k in nodes_of(line, d)]
    if column is None:
        u = [jnp.concatenate([state[k], state[COLUMN + k]], axis=0) for k in at]
    else:
        u = [state[column * COLUMN + k] for k in at]
    near, away = jnp.where(high, u[2], u[0]), jnp.where(high, u[0], u[2])
    slope = edge_slope(near, u[1], away)
    return near, jnp.where(high, slope, -slope)


def put_upright(state, target, high):
    for i in range(5):
        for line in range(9):
            near, slope = edge_of(state, None, i, line, 1, high)
            for row, x in ((0, near), (2, slope)):
                target[9 * i + line, row : row + 1, :] = jnp.where(high, x[3:4], x[0:1])
                target[9 * i + line, row + 1 : row + 2, :] = jnp.where(high, x[7:8], x[4:5])


def pack_wide(state, tables, wide_a, wide_b):
    odd, n = lax.rem(lax.axis_index("wide"), 2), lax.axis_index("narrow")

    @pl.when(n == 0)
    def _():
        for target, near in ((wide_a, odd), (wide_b, 1 - odd)):
            first, other = near * COLUMN, (1 - near) * COLUMN
            target[0:COLUMN] = state[pl.ds(first, COLUMN)]
            for m in range(HALF):
                later = min(m + HALF, COLUMN - 1)
                target[COLUMN + m, 0:2, :] = state[other + m, 0:2, :]
                target[COLUMN + m, 2:4, :] = state[other + later, 0:2, :]
            own, swapped = tables[...], jnp.concatenate([tables[2:4], tables[0:2]], axis=0)
            target[WIDE_TILES - 1] = jnp.where(near == 0, own, swapped)

    @pl.when(n > 0)
    def _():
        put_upright(state, wide_b, lax.rem(n, 2) == 1)
        for i in range(5):
            for line in range(9):
                near, slope = edge_of(state, 1 - odd, i, line, 0, odd == 0)
                wide_a[9 * i + line], wide_a[NARROW_TILES + 9 * i + line] = near, slope


def pack_rest(state, narrow, far_a, far_b):
    w, n = lax.axis_index("wide"), lax.axis_index("narrow")
    odd, low_pair = lax.rem(w, 2), (lax.rem(w, 4) < 2).astype(jnp.int32)
    put_upright(state, narrow, lax.rem(n, 2) == 0)

    @pl.when(n == 0)
    def _():
        for target, column in ((far_a, 1 - low_pair), (far_b, low_pair)):
            for i in range(5):
                for line in range(9):
                    for k, x in zip((0, 45), edge_of(state, column, i, line, 0, column == 1)):
                        m = k + 9 * i + line
                        target[m // 4, m % 4 : m % 4 + 1, :] = x[0:1]

    @pl.when(n > 0)
    def _():
        for i in range(5):
            for line in range(9):
                m = 9 * i + line
                far_a[m], far_b[m] = edge_of(state, odd, i, line, 0, odd == 1)


def pressure_of(v, inverse):
    return 0.4 * (v[4] - 0.5 * (v[1] * v[1] + v[2] * v[2] + v[3] * v[3]) * inverse)


def flux(v, d, inverse, pressure, sound):
    speed = v[1 + d] * inverse
    out = [v[1 + d], v[1] * speed, v[2] * speed, v[3] * speed, (v[4] + pressure) * speed]
    out[1 + d] = out[1 + d] + pressure
    return out, jnp.abs(speed) + sound


def thermo(v):
    inverse = 1.0 / v[0]
    pressure = pressure_of(v, inverse)
    return inverse, pressure, jnp.sqrt(1.4 * pressure * inverse)


def load(ref, node):
    return [ref[i, node] for i in range(5)]


def fill(vector, nodes, pre):
    for n in range(NODES):
        v = [vector(27 * i + n) for i in range(5)]
        for i in range(5):
            nodes[i, n] = v[i]
        for j, x in enumerate(thermo(v)):
            pre[j, n] = x


def interior(nodes, pre, rate, height):
    sub = sublane()
    inner_x = lax.rem(sub, 2 * height) >= height
    inner_y = lax.rem(sub, height) > 0
    moves = (
        (lambda x: roll(x, height), lambda x: roll(x, -height), inner_x),
        (lambda x: roll(x, 1), lambda x: roll(x, -1), inner_y),
        (lambda x: pltpu.roll(x, 1, 1), lambda x: pltpu.roll(x, 127, 1), None),
    )
    for d in range(3):
        ahead, back, inner = moves[d]

        def body(line, carry, d=d, ahead=ahead, back=back, inner=inner):
            at = nodes_of(line, d)
            v = [load(nodes, n) for n in at]
            f, speeds = zip(*[flux(v[k], d, *[pre[j, at[k]] for j in range(3)]) for k in range(3)])
            speed = 0.5 * jnp.maximum(speeds[0], ahead(speeds[2]))
            for i in range(5):
                a, b, c = v[0][i], v[1][i], v[2][i]
                g_low = f[0][i] + 0.1 * edge_slope(a, b, c)
                g_mid = f[1][i] - 0.05 * (c - a)
                g_high = f[2][i] - 0.1 * edge_slope(c, b, a)
                jump = a - ahead(c)
                lift = 0.075 * jump
                face = 1.5 * (ahead(g_high) + g_low) - 3.0 * (speed * jump) - 3.0 * lift
                if inner is not None:
                    face, lift = jnp.where(inner, face, 0.0), jnp.where(inner, lift, 0.0)
                face_up, lift_up = back(face), back(lift)
                first = face - lift_up - 1.5 * g_low - 2.0 * g_mid + 0.5 * g_high
                second = lift_up - lift + 0.5 * (g_low - g_high)
                third = lift - face_up - 0.5 * g_low + 2.0 * g_mid + 1.5 * g_high
                for n, x in zip(at, (first, second, third)):
                    rate[i, n] = x if d == 0 else rate[i, n] + x
            return carry

        for line in range(9):
            body(line, 0)


def outer(nodes, rate, d, lower, active, halo, fresh=False, beside=None):
    turn = jnp.where(lower, 1.0, -1.0)
    for line in range(9):
        at = nodes_of(line, d)
        v = [load(nodes, n) for n in at]
        near = [jnp.where(lower, a, c) for a, c in zip(v[0], v[2])]
        away = [jnp.where(lower, c, a) for a, c in zip(v[0], v[2])]
        slope = [-turn * edge_slope(*x) for x in zip(near, v[1], away)]
        other, other_slope = halo(line, near, slope)
        f, speed = flux(near, d, *thermo(near))
        f_other, speed_other = flux(other, d, *thermo(other))
        half = 0.5 * jnp.maximum(speed, speed_other)
        for i in range(5):
            jump = turn * (near[i] - other[i])
            face = (
                0.5 * (f[i] + f_other[i])
                - half * jump
                - 0.05 * (slope[i] + other_slope[i])
                - 0.15 * jump
            )
            edge = jnp.where(active, turn * (3.0 * face + 0.225 * jump), 0.0)
            lift = jnp.where(active, turn * (0.075 * jump), 0.0)
            parts = (jnp.where(lower, edge, lift), -lift, jnp.where(lower, lift, edge))
            for n, x in zip(at, parts):
                rate[i, n] = x if fresh else rate[i, n] + x
            if beside is not None:
                beside(i, at, edge, lift)


def mirrored(v):
    return [v[0], -v[1], -v[2], -v[3], v[4]]


def upright_traces(line, near, slope, pick, wall, top):
    sub = sublane()
    first_column, lowest = sub < 4, lax.rem(sub, 4) == 0
    edge = jnp.logical_or(wall, top)
    other, other_slope = [], []
    image = mirrored(near)
    for i in range(5):
        low, high = pick(9 * i + line)

        def spread(row):
            return jnp.where(
                first_column,
                jnp.where(lowest, low[row : row + 1], high[row : row + 1]),
                jnp.where(lowest, low[row + 1 : row + 2], high[row + 1 : row + 2]),
            )

        other.append(jnp.where(wall, image[i], jnp.where(top, near[i], spread(0))))
        other_slope.append(jnp.where(edge, slope[i], spread(2)))
    return other, other_slope


def wall_kernel(nodes, rate_in, narrow, rate):
    rate[...] = rate_in[...]
    height = lax.rem(sublane(), 4)
    lowest, none = height == 0, height < 0

    def upright(line, near, slope):
        return upright_traces(line, near, slope, lambda m: (narrow[m], narrow[m]), lowest, none)

    @pl.when(lax.axis_index("narrow") == 0)
    def _():
        outer(nodes, rate, 1, lowest, jnp.logical_or(lowest, height == 3), upright)


def inner_kernel(state, nodes, rate, pre):
    fill(lambda k: jnp.concatenate([state[k], state[COLUMN + k]], axis=0), nodes, pre)
    interior(nodes, pre, rate, 4)


def below_rows(x):
    return [6.0 * x[0] - 8.0 * x[1] + 3.0 * x[2], 3.0 * x[0] - 3.0 * x[1] + x[2], x[0]]


def above_rows(x):
    return [x[2], x[0] - 3.0 * x[1] + 3.0 * x[2], 3.0 * x[0] - 8.0 * x[1] + 6.0 * x[2]]


def below_columns(x):
    return [6.0 * x[0] + 3.0 * x[1] + x[2], -8.0 * x[0] - 3.0 * x[1], 3.0 * x[0] + x[1]]


def above_columns(x):
    return [x[1] + 3.0 * x[2], -3.0 * x[1] - 8.0 * x[2], x[0] + 3.0 * x[1] + 6.0 * x[2]]


BELOW = ((6.0, -8.0, 3.0), (3.0, -3.0, 1.0), (1.0, 0.0, 0.0))
ABOVE = ((0.0, 0.0, 1.0), (1.0, -3.0, 3.0), (3.0, -8.0, 6.0))
ENDS = (1.0 / 3.0, 4.0 / 3.0, 1.0 / 3.0)
PAIRS = tuple((i, j) for i in range(3) for j in range(i + 1))
BELOW_DIAGONAL = tuple((r, j) for j in range(9) for r in range(j + 1, 9))


def weight(a, b, c):
    return ENDS[a] * ENDS[b] * ENDS[c]


def combine(table, x, i, j):
    total = None
    for k in range(3):
        factor = table[k][i] * table[k][j]
        if factor != 0.0:
            term = x[k] if factor == 1.0 else factor * x[k]
            total = term if total is None else total + term
    return total


def source_of(x, k):
    return (roll(x, -1), x, roll(x, 1))[k]


def masks_of(code):
    return [(code == float(k)).astype(jnp.float32) for k in (1, 2, 3)]


def factorize(code, rule, fractions, taken, scaled, factor):
    index = lax.broadcasted_iota(jnp.int32, (64, 128), 0).astype(jnp.float32)
    onehot = jnp.concatenate(
        [(index == rule[j : j + 1, :]).astype(jnp.float32) for j in range(8)], axis=1
    )
    shares = lax.dot_general(
        fractions[...],
        onehot,
        (((1,), (0,)), ((), ())),
        precision=lax.Precision.HIGHEST,
        preferred_element_type=jnp.float32,
    )
    for j in range(8):
        taken[32 * j : 32 * j + 27, :] = shares[:, 128 * j : 128 * j + 128]
    is_cut = code > 0.0
    masks = masks_of(code)
    for c in range(3):
        inner = [[None] * 3 for _ in range(3)]
        for a in range(3):
            parts = [[], [], []]
            for b in range(3):
                n = 9 * a + 3 * b + c
                amount = jnp.where(is_cut, weight(a, b, c) * taken[pl.ds(n, 8, stride=32), :], 0.0)
                scaled[n] = amount
                for k in range(3):
                    parts[k].append(source_of(jnp.where(masks[k] > 0.0, amount, 0.0), k))
            for k in range(3):
                inner[k][a] = {p: combine(BELOW, parts[k], *p) for p in PAIRS}
        matrix = {}
        for row in range(9):
            for column in range(row + 1):
                (a, b), (a2, b2) = divmod(row, 3), divmod(column, 3)
                p = (max(b, b2), min(b, b2))
                total = combine(ABOVE, [inner[0][i][p] for i in range(3)], a, a2)
                third = combine(BELOW, [inner[2][i][p] for i in range(3)], a, a2)
                if third is not None:
                    total = third if total is None else total + third
                if a == a2:
                    total = total + inner[1][a][p]
                if row == column:
                    total = total + weight(a, b, c)
                matrix[row, column] = total
        for j in range(9):
            inverse = 1.0 / matrix[j, j]
            factor[c, 36 + j] = inverse
            lower = {r: matrix[r, j] * inverse for r in range(j + 1, 9)}
            for r in range(j + 1, 9):
                factor[c, BELOW_DIAGONAL.index((r, j))] = lower[r]
                for s in range(j + 1, r + 1):
                    matrix[r, s] = matrix[r, s] - lower[r] * matrix[s, j]


def edge_kernel(
    nodes,
    rate_in,
    wide_a,
    wide_b,
    narrow,
    tables,
    fractions,
    rate,
    strip_nodes,
    codes,
    right,
    ends,
    factor,
    taken,
    strip_pre,
    strip_rate,
    scaled,
):
    rate[...] = rate_in[...]
    w, n = lax.axis_index("wide"), lax.axis_index("narrow")
    odd = lax.rem(w, 2) == 1
    odd_n, at_bottom, at_top = lax.rem(n, 2) == 1, n == 0, n == lax.axis_size("narrow") - 1
    sub = sublane()
    first_column = sub < 4
    height = lax.rem(sub, 4)

    def sides(k):
        a, b = wide_a[k], wide_b[k]
        return jnp.where(odd, b, a), jnp.where(odd, a, b)

    def both_sides(k_left, k_right):
        return jnp.concatenate([sides(k_left)[0], sides(k_right)[1]], axis=0)

    def across(line, near, slope):
        at = nodes_of(line, 0)
        u = [
            [both_sides(27 * i + at[2 - j], 27 * i + at[j]) for i in range(5)] for j in range(3)
        ]
        other = [edge_slope(*x) for x in zip(*u)]
        return u[0], [jnp.where(first_column, x, -x) for x in other]

    lowest, none = height == 0, height < 0
    top = jnp.logical_and(height == 3, at_top)

    def pick(m):
        a, b = narrow[m], wide_b[m]
        return jnp.where(odd_n, a, b), jnp.where(odd_n, b, a)

    def upright(line, near, slope):
        return upright_traces(line, near, slope, pick, none, top)

    @pl.when(n > 0)
    def _():
        outer(nodes, rate, 1, lowest, jnp.logical_or(lowest, height == 3), upright)

    @pl.when(at_bottom)
    def _():
        def strip_vector(k):
            left, right = sides(k)
            tile, row = (COLUMN + k, 0) if k < HALF else (COLUMN + k - HALF, 2)
            far_left, far_right = sides(tile)
            return jnp.concatenate(
                [far_left[row : row + 2], left[0:2], right[0:2], far_right[row : row + 2]], axis=0
            )

        fill(strip_vector, strip_nodes, strip_pre)
        interior(strip_nodes, strip_pre, strip_rate, 2)
        middle = jnp.logical_and(sub >= 2, sub < 6)

        def beside(i, at, edge, lift):
            edge, lift = [jnp.where(first_column, roll(x, 2), x) for x in (edge, lift)]
            edge, lift = [jnp.where(middle, x, 0.0) for x in (edge, lift)]
            parts = (jnp.where(first_column, lift, edge), -lift, jnp.where(first_column, edge, lift))
            for n, x in zip(at, parts):
                strip_rate[i, n] -= x

        outer(nodes, rate, 0, first_column, sub >= 0, across, beside=beside)
        strip_lowest = lax.rem(sub, 2) == 0

        def above(k):
            x = both_sides(k, k)
            return jnp.where(first_column, roll(x, 1), roll(x, -1))

        def strip_upright(line, near, slope):
            at = nodes_of(line, 1)
            u = [[above(27 * i + m) for i in range(5)] for m in at]
            other = [-edge_slope(*x) for x in zip(*u)]
            image = mirrored(near)
            return (
                [jnp.where(strip_lowest, x, y) for x, y in zip(image, u[0])],
                [jnp.where(strip_lowest, x, y) for x, y in zip(slope, other)],
            )

        outer(strip_nodes, strip_rate, 1, strip_lowest, sub >= 0, strip_upright)

        from_left, from_right = sides(WIDE_TILES - 1)

        def in_row(row):
            parts = [from_left[row + 2 : row + 3]] * 2 + [from_left[row : row + 1]]
            parts += [tables[row : row + 1], tables[row + 2 : row + 3]]
            parts += [from_right[row : row + 1]] + [from_right[row + 2 : row + 3]] * 2
            return jnp.concatenate(parts, axis=0)

        code = in_row(0)
        codes[...] = code
        factorize(code, in_row(1), fractions, taken, scaled, factor)
        cut_right(code, rate, strip_rate, scaled, right, ends)


def cut_right(code, rate, strip_rate, scaled, right, ends):
    sub = sublane()
    masks = [code == float(k) for k in (1, 2, 3)]
    odd_sublane = lax.rem(sub, 2) == 1

    def in_row(i, n):
        s, m = strip_rate[i, n], rate[i, n]
        s = jnp.where(odd_sublane, roll(s, 1), s)
        return jnp.where(sub == 3, roll(m, 3), jnp.where(sub == 4, m, s))

    def in_second_row(i, n):
        s, m = strip_rate[i, n], rate[i, n]
        s = jnp.where(sub == 2, roll(s, -1), s)
        return jnp.where(sub == 3, roll(m, 2), jnp.where(sub == 4, roll(m, -1), s))

    left_end = jnp.logical_and(sub == 1, masks[2])
    right_end = jnp.logical_and(sub == 6, masks[0])
    for n in range(NODES):
        c = scaled[n]
        ends[n] = roll(jnp.where(left_end, c, 0.0), -1) + jnp.where(right_end, c, 0.0)
    for c in range(3):
        for i in range(5):
            y = []
            for a in range(3):
                at = [9 * a + 3 * b + c for b in range(3)]
                y.append(below_columns([scaled[n] * in_row(i, n) for n in at]))
            for b in range(3):
                line = [y[a][b] for a in range(3)]
                parts = (above_columns(line), line, below_columns(line))
                for a in range(3):
                    n = 9 * a + 3 * b + c
                    total = weight(a, b, c) * in_second_row(i, n)
                    for k in range(3):
                        total += source_of(jnp.where(masks[k], parts[k][a], 0.0), k)
                    right[i, n] = total


def cut_solve(code, rate, extra, ends, right, factor, done):
    sub = sublane()
    is_cut = code > 0.0
    masks = [code == float(k) for k in (1, 2, 3)]
    m_float = masks_of(code)
    has_target = source_of(m_float[0], 0) + m_float[1] + source_of(m_float[2], 2)
    cut = is_cut.astype(jnp.float32)
    cut_low = jnp.logical_and(sub == 0, roll(cut, -3) > 0.0)
    cut_high = jnp.logical_and(sub == 4, is_cut)
    target_low = jnp.logical_and(sub == 1, roll(has_target, -2) > 0.0)
    target_high = jnp.logical_and(sub == 5, roll(has_target, 1) > 0.0)
    for c in range(3):
        x = [[None] * 9 for _ in range(5)]
        for i in range(5):
            y = []
            for a in range(3):
                at = [9 * a + 3 * b + c for b in range(3)]
                y.append(below_columns([ends[n] * extra[i, n] for n in at]))
            for b in range(3):
                line = [y[a][b] for a in range(3)]
                for a, (p, q) in enumerate(zip(below_columns(line), above_columns(line))):
                    p = jnp.where(sub == 0, p, q)
                    x[i][3 * a + b] = right[i, 9 * a + 3 * b + c] + (roll(p, 2) + roll(p, -1))
        for j in range(9):
            for r in range(j + 1, 9):
                f = factor[c, BELOW_DIAGONAL.index((r, j))]
                for i in range(5):
                    x[i][r] = x[i][r] - f * x[i][j]
        for j in range(9):
            f = factor[c, 36 + j]
            for i in range(5):
                x[i][j] = x[i][j] * f
        for r in range(8, 0, -1):
            for j in range(r):
                f = factor[c, BELOW_DIAGONAL.index((r, j))]
                for i in range(5):
                    x[i][j] = x[i][j] - f * x[i][r]
        for i in range(5):
            y = []
            for a in range(3):
                line = [
                    jnp.where(masks[0], roll(s, 1), jnp.where(masks[2], roll(s, -1), s))
                    for s in x[i][3 * a : 3 * a + 3]
                ]
                y.append(below_rows(line))
            for b in range(3):
                line = [y[a][b] for a in range(3)]
                one, three = above_rows(line), below_rows(line)
                for a in range(3):
                    n = 9 * a + 3 * b + c
                    update = jnp.where(masks[0], one[a], jnp.where(masks[2], three[a], line[a]))
                    target = x[i][3 * a + b]
                    m = rate[i, n]
                    m = jnp.where(cut_low, roll(update, -3), jnp.where(cut_high, update, m))
                    m = jnp.where(target_low, roll(target, -2), m)
                    done(i, n, jnp.where(target_high, roll(target, 1), m))


def last_kernel(
    start,
    nodes,
    rate,
    strip_nodes,
    codes,
    right,
    ends,
    factor,
    wide_a,
    far_a,
    far_b,
    out,
    extra,
    staged,
    sem,
):
    w, n = lax.axis_index("wide"), lax.axis_index("narrow")
    odd, low_pair = lax.rem(w, 2) == 1, lax.rem(w, 4) < 2
    sub = sublane()
    first_column = sub < 4

    def finish(i, n, change):
        k = NODES * i + n
        value = 0.25 * nodes[i, n] + 0.0075 * change
        staged[k] = 0.75 * start[k] + value[0:4]
        staged[COLUMN + k] = 0.75 * start[COLUMN + k] + value[4:8]

    @pl.when(n == 0)
    def _():
        use_far = jnp.logical_xor(first_column, jnp.logical_not(low_pair))

        def value(m):
            tile, row = m // 4, pl.ds(m % 4, 1)
            return jnp.where(use_far, far_a[tile, row, :], far_b[tile, row, :])

        def beyond(line, near, slope):
            at = [9 * i + line for i in range(5)]
            return [value(m) for m in at], [value(45 + m) for m in at]

        outermost = jnp.logical_or(sub == 0, sub == 6)
        outer(strip_nodes, extra, 0, lax.rem(sub, 4) < 2, outermost, beyond, fresh=True)
        cut_solve(codes[...], rate, extra, ends, right, factor, finish)

    def across(line, near, slope):
        def value(a, b):
            return jnp.concatenate([jnp.where(odd, b, a), jnp.where(odd, a, b)], axis=0)

        at = [9 * i + line for i in range(5)]
        return (
            [value(far_a[m], wide_a[m]) for m in at],
            [value(far_b[m], wide_a[NARROW_TILES + m]) for m in at],
        )

    @pl.when(n > 0)
    def _():
        outer(nodes, extra, 0, first_column, sub >= 0, across, fresh=True)
        for k in range(COLUMN):
            i, m = divmod(k, NODES)
            finish(i, m, rate[i, m] + extra[i, m])

    copy = pltpu.make_async_copy(staged, out, sem)
    copy.start()
    copy.wait()


def as_tiles(x):
    return jnp.transpose(x, (0, 2, 3, 1, 4)).reshape(2 * COLUMN, 4, 128)


def from_tiles(x):
    return jnp.transpose(x.reshape(2, 5, NODES, 4, 128), (0, 3, 1, 2, 4))


def device_step(wide, narrow, section_start, section_state, cut_code, cut_rule, rule_fractions):
    f32 = jnp.float32

    def call(kernel, name, shapes, operands, scratch=(), flops=0, out_space=pltpu.VMEM):
        vmem = pl.BlockSpec(memory_space=pltpu.VMEM)
        cost = pl.CostEstimate(flops=flops, bytes_accessed=0, transcendentals=0) if flops else None
        return pl.pallas_call(
            kernel,
            name=name,
            out_shape=[jax.ShapeDtypeStruct(s, f32) for s in shapes],
            in_specs=[vmem] * len(operands),
            out_specs=[pl.BlockSpec(memory_space=out_space)] * len(shapes),
            scratch_shapes=list(scratch),
            cost_estimate=cost,
            compiler_params=pltpu.CompilerParams(vmem_limit_bytes=8 * 2**20),
        )(*operands)

    state, start = as_tiles(section_state), as_tiles(section_start)
    wide_shape, narrow_shape = (WIDE_TILES, 4, 128), (NARROW_TILES, 4, 128)
    tables = jnp.stack([cut_code, cut_rule], axis=1).reshape(4, 128).astype(f32)
    mine_a, mine_b = call(pack_wide, "pack_wide", [wide_shape] * 2, (state, tables))
    up, far_a, far_b = call(pack_rest, "pack_rest", [narrow_shape] * 3, (state,))

    both = ("wide", "narrow")
    half = wide // 2
    cross = swaps([(2 * j + 1, (2 * j + 2) % wide) for j in range(half)])
    inside = swaps([(2 * j, 2 * j + 1) for j in range(half)])
    far_inside = swaps([(4 * j + k, 4 * j + 2 + k) for j in range(wide // 4) for k in (0, 1)])
    far_cross = [(4 * j + 2 + k, (4 * j + 4 + k) % wide) for j in range(wide // 4) for k in (0, 1)]
    far_cross = swaps(far_cross)
    even = swaps([(2 * j, 2 * j + 1) for j in range(narrow // 2)])
    between = swaps([(2 * j + 1, 2 * j + 2) for j in range(narrow // 2 - 1)])
    unused = swaps([(16 * j + k, 16 * j + 8 + k) for j in range(wide // 16) for k in range(8)])

    def along_wide(pairs, *rows):
        return [(narrow * a + n, narrow * b + n) for a, b in pairs for n in rows]

    def along_narrow(pairs):
        return [(narrow * w + a, narrow * w + b) for w in range(wide) for a, b in pairs]

    others = range(1, narrow)
    wide_a = lax.ppermute(mine_a, both, along_wide(cross, 0) + along_wide(inside, *others))
    wide_b = lax.ppermute(
        mine_b,
        both,
        along_wide(inside, 0) + along_narrow(between) + along_wide(unused, narrow - 1),
    )
    narrow_got = lax.ppermute(up, both, along_narrow(even))
    far_a = lax.ppermute(far_a, both, along_wide(far_cross, 0) + along_wide(cross, *others))
    far_b = lax.ppermute(far_b, both, along_wide(far_inside, 0) + along_wide(cross, *others))

    full = (5, NODES, 8, 128)
    thermal = pltpu.VMEM((3, NODES, 8, 128), f32)
    nodes, rate = call(inner_kernel, "inner", [full, full], (state,), [thermal], flops=10**9)
    (rate,) = call(wall_kernel, "wall", [full], (nodes, rate, narrow_got), flops=10**8)
    rate, *strip = call(
        edge_kernel,
        "edge",
        [full, full, (8, 128), full, (NODES, 8, 128), (3, 45, 8, 128)],
        (nodes, rate, wide_a, wide_b, narrow_got, tables, rule_fractions.T),
        scratch=[
            pltpu.VMEM((8 * 32, 128), f32),
            thermal,
            pltpu.VMEM(full, f32),
            pltpu.VMEM((NODES, 8, 128), f32),
        ],
        flops=10**9,
    )
    (out,) = call(
        last_kernel,
        "last",
        [(2 * COLUMN, 4, 128)],
        (start, nodes, rate, *strip, wide_a, far_a, far_b),
        scratch=[
            pltpu.VMEM(full, f32),
            pltpu.VMEM((2 * COLUMN, 4, 128), f32),
            pltpu.SemaphoreType.DMA(()),
        ],
        out_space=pl.ANY,
    )
    return from_tiles(out)


def solution(mesh):
    return jax.shard_map(
        functools.partial(device_step, mesh.shape["wide"], mesh.shape["narrow"]),
        mesh=mesh,
        in_specs=(
            P("wide", "narrow", None, None, None),
            P("wide", "narrow", None, None, None),
            P("wide", None),
            P("wide", None),
            P(),
        ),
        out_specs=P("wide", "narrow", None, None, None),
        check_vma=False,
    )
```

```python
import functools

import jax
import jax.numpy as jnp
from jax import lax
from jax.experimental import pallas as pl
from jax.experimental.pallas import tpu as pltpu
from jax.sharding import PartitionSpec as P

NODES = 27
COLUMN = 5 * NODES
HALF = 68
WIDE_TILES = COLUMN + HALF + 1
NARROW_TILES = 45
FAR_TILES = 24
SIDE_TILES = 2 * NARROW_TILES


def swaps(pairs):
    return [p for a, b in pairs for p in ((a, b), (b, a))]


def nodes_of(line, d):
    base = (line, 9 * (line // 3) + line % 3, 3 * line)[d]
    return [base + (9, 3, 1)[d] * k for k in range(3)]


def sublane():
    return lax.broadcasted_iota(jnp.int32, (8, 128), 0)


def roll(x, shift):
    return pltpu.roll(x, shift % 8, 0)


def edge_slope(near, middle, away):
    return 1.5 * near - 2.0 * middle + 0.5 * away


def edge_of(state, column, i, line, d, high):
    at = [27 * i + k for k in nodes_of(line, d)]
    if column is None:
        u = [jnp.concatenate([state[k], state[COLUMN + k]], axis=0) for k in at]
    else:
        u = [state[column * COLUMN + k] for k in at]
    near, away = jnp.where(high, u[2], u[0]), jnp.where(high, u[0], u[2])
    slope = edge_slope(near, u[1], away)
    return near, jnp.where(high, slope, -slope)


def put_upright(state, target, high):
    for i in range(5):
        for line in range(9):
            near, slope = edge_of(state, None, i, line, 1, high)
            for row, x in ((0, near), (2, slope)):
                target[9 * i + line, row : row + 1, :] = jnp.where(high, x[3:4], x[0:1])
                target[9 * i + line, row + 1 : row + 2, :] = jnp.where(high, x[7:8], x[4:5])


def begin_kernel(zero):
    zero[...] = jnp.zeros_like(zero)


def pack_wide(state, code, rule, zero, wide_a, wide_b, tables):
    del zero
    odd, n = lax.rem(lax.axis_index("wide"), 2), lax.axis_index("narrow")
    for row, table in ((0, code), (1, rule)):
        for column in range(2):
            line = table[column : column + 1, :].astype(jnp.float32)
            tables[2 * column + row : 2 * column + row + 1, :] = line

    @pl.when(n == 0)
    def _():
        for target, near in ((wide_a, odd), (wide_b, 1 - odd)):
            first, other = near * COLUMN, (1 - near) * COLUMN
            target[0:COLUMN] = state[pl.ds(first, COLUMN)]
            for m in range(HALF):
                later = min(m + HALF, COLUMN - 1)
                target[COLUMN + m, 0:2, :] = state[other + m, 0:2, :]
                target[COLUMN + m, 2:4, :] = state[other + later, 0:2, :]
            own, swapped = tables[...], jnp.concatenate([tables[2:4], tables[0:2]], axis=0)
            target[WIDE_TILES - 1] = jnp.where(near == 0, own, swapped)

    @pl.when(n > 0)
    def _():
        put_upright(state, wide_b, lax.rem(n, 2) == 1)
        for i in range(5):
            for line in range(9):
                near, slope = edge_of(state, 1 - odd, i, line, 0, odd == 0)
                wide_a[9 * i + line], wide_a[NARROW_TILES + 9 * i + line] = near, slope


def pack_narrow(state, narrow):
    put_upright(state, narrow, lax.rem(lax.axis_index("narrow"), 2) == 0)


def pack_far(state, far_a, far_b):
    w, n = lax.axis_index("wide"), lax.axis_index("narrow")
    odd, low_pair = lax.rem(w, 2), (lax.rem(w, 4) < 2).astype(jnp.int32)

    @pl.when(n == 0)
    def _():
        for target, column in ((far_a, 1 - low_pair), (far_b, low_pair)):
            for i in range(5):
                for line in range(9):
                    for k, x in zip((0, 45), edge_of(state, column, i, line, 0, column == 1)):
                        m = k + 9 * i + line
                        target[m // 4, m % 4 : m % 4 + 1, :] = x[0:1]

    @pl.when(n > 0)
    def _():
        for i in range(5):
            for line in range(9):
                near, slope = edge_of(state, odd, i, line, 0, odd == 1)
                for m, x in ((9 * i + line, near), (NARROW_TILES + 9 * i + line, slope)):
                    if m < FAR_TILES:
                        far_a[m] = x
                    else:
                        far_b[m - FAR_TILES] = x


def pressure_of(v, inverse):
    return 0.4 * (v[4] - 0.5 * (v[1] * v[1] + v[2] * v[2] + v[3] * v[3]) * inverse)


def flux(v, d, inverse, pressure, sound):
    speed = v[1 + d] * inverse
    out = [v[1 + d], v[1] * speed, v[2] * speed, v[3] * speed, (v[4] + pressure) * speed]
    out[1 + d] = out[1 + d] + pressure
    return out, jnp.abs(speed) + sound


def thermo(v):
    inverse = 1.0 / v[0]
    pressure = pressure_of(v, inverse)
    return inverse, pressure, jnp.sqrt(1.4 * pressure * inverse)


def load(ref, node):
    return [ref[i, node] for i in range(5)]


def fill(vector, nodes, pre):
    for n in range(NODES):
        v = [vector(27 * i + n) for i in range(5)]
        for i in range(5):
            nodes[i, n] = v[i]
        for j, x in enumerate(thermo(v)):
            pre[j, n] = x


def interior(nodes, pre, rate, height):
    sub = sublane()
    inner_x = lax.rem(sub, 2 * height) >= height
    inner_y = lax.rem(sub, height) > 0
    moves = (
        (lambda x: roll(x, height), lambda x: roll(x, -height), inner_x),
        (lambda x: roll(x, 1), lambda x: roll(x, -1), inner_y),
        (lambda x: pltpu.roll(x, 1, 1), lambda x: pltpu.roll(x, 127, 1), None),
    )
    for d in range(3):
        ahead, back, inner = moves[d]

        def body(line, carry, d=d, ahead=ahead, back=back, inner=inner):
            at = nodes_of(line, d)
            v = [load(nodes, n) for n in at]
            f, speeds = zip(*[flux(v[k], d, *[pre[j, at[k]] for j in range(3)]) for k in range(3)])
            speed = 1.5 * jnp.maximum(speeds[0], ahead(speeds[2])) + 0.225
            for i in range(5):
                a, b, c = v[0][i], v[1][i], v[2][i]
                bend = 0.5 * (a + c) - 2.0 * b
                g_low = f[0][i] + 0.1 * (a + bend)
                g_mid = 2.0 * f[1][i] - 0.1 * (c - a)
                g_high = f[2][i] - 0.1 * (c + bend)
                jump = a - ahead(c)
                face = 1.5 * (ahead(g_high) + g_low) - speed * jump
                if inner is not None:
                    face, jump = jnp.where(inner, face, 0.0), jnp.where(inner, jump, 0.0)
                lift = 0.075 * jump
                face_up, lift_up = back(face), back(lift)
                turn = 0.5 * (g_low - g_high)
                above, below = lift_up + turn, lift - turn
                first = face - g_low - g_mid - above
                second = above - lift
                third = below - face_up + g_high + g_mid
                for n, x in zip(at, (first, second, third)):
                    rate[i, n] = x if d == 0 else rate[i, n] + x
            return carry

        for line in range(9):
            body(line, 0)


def outer(nodes, rate, d, lower, active, halo, fresh=False, beside=None):
    turn = jnp.where(lower, 1.0, -1.0)
    face_sign = 1.5 * turn
    for line in range(9):
        at = nodes_of(line, d)
        v = [load(nodes, n) for n in at]
        near = [jnp.where(lower, a, c) for a, c in zip(v[0], v[2])]
        away = [jnp.where(lower, c, a) for a, c in zip(v[0], v[2])]
        slope = [-turn * edge_slope(*x) for x in zip(near, v[1], away)]
        other, other_slope = halo(line, near, slope)
        f, speed = flux(near, d, *thermo(near))
        f_other, speed_other = flux(other, d, *thermo(other))
        speed = 1.5 * jnp.maximum(speed, speed_other) + 0.225
        for i in range(5):
            gap = near[i] - other[i]
            both = f[i] + f_other[i] - 0.1 * (slope[i] + other_slope[i])
            edge = jnp.where(active, face_sign * both - speed * gap, 0.0)
            lift = jnp.where(active, 0.075 * gap, 0.0)
            parts = (jnp.where(lower, edge, lift), -lift, jnp.where(lower, lift, edge))
            for n, x in zip(at, parts):
                rate[i, n] = x if fresh else rate[i, n] + x
            if beside is not None:
                beside(i, at, edge, lift)


def mirrored(v):
    return [v[0], -v[1], -v[2], -v[3], v[4]]


def upright_traces(line, near, slope, pick, wall, top):
    sub = sublane()
    first_column, lowest = sub < 4, lax.rem(sub, 4) == 0
    edge = jnp.logical_or(wall, top)
    other, other_slope = [], []
    image = mirrored(near)
    for i in range(5):
        low, high = pick(9 * i + line)

        def spread(row):
            return jnp.where(
                first_column,
                jnp.where(lowest, low[row : row + 1], high[row : row + 1]),
                jnp.where(lowest, low[row + 1 : row + 2], high[row + 1 : row + 2]),
            )

        other.append(jnp.where(wall, image[i], jnp.where(top, near[i], spread(0))))
        other_slope.append(jnp.where(edge, slope[i], spread(2)))
    return other, other_slope


def wall_kernel(nodes, rate_in, narrow, rate):
    rate[...] = rate_in[...]
    height = lax.rem(sublane(), 4)
    lowest, none = height == 0, height < 0

    def upright(line, near, slope):
        return upright_traces(line, near, slope, lambda m: (narrow[m], narrow[m]), lowest, none)

    @pl.when(lax.axis_index("narrow") == 0)
    def _():
        outer(nodes, rate, 1, lowest, jnp.logical_or(lowest, height == 3), upright)


def inner_kernel(state, nodes, rate, pre):
    fill(lambda k: jnp.concatenate([state[k], state[COLUMN + k]], axis=0), nodes, pre)
    interior(nodes, pre, rate, 4)


def below_rows(x):
    return [6.0 * x[0] - 8.0 * x[1] + 3.0 * x[2], 3.0 * x[0] - 3.0 * x[1] + x[2], x[0]]


def above_rows(x):
    return [x[2], x[0] - 3.0 * x[1] + 3.0 * x[2], 3.0 * x[0] - 8.0 * x[1] + 6.0 * x[2]]


def below_columns(x):
    return [6.0 * x[0] + 3.0 * x[1] + x[2], -8.0 * x[0] - 3.0 * x[1], 3.0 * x[0] + x[1]]


def above_columns(x):
    return [x[1] + 3.0 * x[2], -3.0 * x[1] - 8.0 * x[2], x[0] + 3.0 * x[1] + 6.0 * x[2]]


BELOW = ((6.0, -8.0, 3.0), (3.0, -3.0, 1.0), (1.0, 0.0, 0.0))
ABOVE = ((0.0, 0.0, 1.0), (1.0, -3.0, 3.0), (3.0, -8.0, 6.0))
ENDS = (1.0 / 3.0, 4.0 / 3.0, 1.0 / 3.0)
PAIRS = tuple((i, j) for i in range(3) for j in range(i + 1))
BELOW_DIAGONAL = tuple((r, j) for j in range(9) for r in range(j + 1, 9))


def weight(a, b, c):
    return ENDS[a] * ENDS[b] * ENDS[c]


def combine(table, x, i, j):
    total = None
    for k in range(3):
        factor = table[k][i] * table[k][j]
        if factor != 0.0:
            term = x[k] if factor == 1.0 else factor * x[k]
            total = term if total is None else total + term
    return total


def source_of(x, k):
    return (roll(x, -1), x, roll(x, 1))[k]


def masks_of(code):
    return [(code == float(k)).astype(jnp.float32) for k in (1, 2, 3)]


def factorize(code, rule, fractions, taken, scaled, factor):
    index = lax.broadcasted_iota(jnp.int32, (64, 128), 0).astype(jnp.float32)
    onehot = jnp.concatenate(
        [(index == rule[j : j + 1, :]).astype(jnp.float32) for j in range(8)], axis=1
    )
    shares = lax.dot_general(
        fractions[...],
        onehot,
        (((1,), (0,)), ((), ())),
        precision=lax.Precision.HIGHEST,
        preferred_element_type=jnp.float32,
    )
    for j in range(8):
        taken[32 * j : 32 * j + 27, :] = shares[:, 128 * j : 128 * j + 128]
    is_cut = code > 0.0
    masks = masks_of(code)
    for c in range(3):
        inner = [[None] * 3 for _ in range(3)]
        for a in range(3):
            parts = [[], [], []]
            for b in range(3):
                n = 9 * a + 3 * b + c
                amount = jnp.where(is_cut, weight(a, b, c) * taken[pl.ds(n, 8, stride=32), :], 0.0)
                scaled[n] = amount
                for k in range(3):
                    parts[k].append(source_of(jnp.where(masks[k] > 0.0, amount, 0.0), k))
            for k in range(3):
                inner[k][a] = {p: combine(BELOW, parts[k], *p) for p in PAIRS}
        matrix = {}
        for row in range(9):
            for column in range(row + 1):
                (a, b), (a2, b2) = divmod(row, 3), divmod(column, 3)
                p = (max(b, b2), min(b, b2))
                total = combine(ABOVE, [inner[0][i][p] for i in range(3)], a, a2)
                third = combine(BELOW, [inner[2][i][p] for i in range(3)], a, a2)
                if third is not None:
                    total = third if total is None else total + third
                if a == a2:
                    total = total + inner[1][a][p]
                if row == column:
                    total = total + weight(a, b, c)
                matrix[row, column] = total
        for j in range(9):
            inverse = 1.0 / matrix[j, j]
            factor[c, 36 + j] = inverse
            lower = {r: matrix[r, j] * inverse for r in range(j + 1, 9)}
            for r in range(j + 1, 9):
                factor[c, BELOW_DIAGONAL.index((r, j))] = lower[r]
                for s in range(j + 1, r + 1):
                    matrix[r, s] = matrix[r, s] - lower[r] * matrix[s, j]


def edge_kernel(
    nodes,
    rate_in,
    wide_a,
    wide_b,
    narrow,
    tables,
    fractions,
    start,
    rate,
    strip_nodes,
    codes,
    right,
    ends,
    factor,
    taken,
    strip_pre,
    strip_rate,
    scaled,
):
    del start
    rate[...] = rate_in[...]
    w, n = lax.axis_index("wide"), lax.axis_index("narrow")
    odd = lax.rem(w, 2) == 1
    odd_n, at_bottom, at_top = lax.rem(n, 2) == 1, n == 0, n == lax.axis_size("narrow") - 1
    sub = sublane()
    first_column = sub < 4
    height = lax.rem(sub, 4)

    def sides(k):
        a, b = wide_a[k], wide_b[k]
        return jnp.where(odd, b, a), jnp.where(odd, a, b)

    def both_sides(k_left, k_right):
        return jnp.concatenate([sides(k_left)[0], sides(k_right)[1]], axis=0)

    def across(line, near, slope):
        at = nodes_of(line, 0)
        u = [
            [both_sides(27 * i + at[2 - j], 27 * i + at[j]) for i in range(5)] for j in range(3)
        ]
        other = [edge_slope(*x) for x in zip(*u)]
        return u[0], [jnp.where(first_column, x, -x) for x in other]

    lowest, none = height == 0, height < 0
    top = jnp.logical_and(height == 3, at_top)

    def pick(m):
        a, b = narrow[m], wide_b[m]
        return jnp.where(odd_n, a, b), jnp.where(odd_n, b, a)

    def upright(line, near, slope):
        return upright_traces(line, near, slope, pick, none, top)

    @pl.when(n > 0)
    def _():
        outer(nodes, rate, 1, lowest, jnp.logical_or(lowest, height == 3), upright)

    @pl.when(at_bottom)
    def _():
        def strip_vector(k):
            left, right = sides(k)
            tile, row = (COLUMN + k, 0) if k < HALF else (COLUMN + k - HALF, 2)
            far_left, far_right = sides(tile)
            return jnp.concatenate(
                [far_left[row : row + 2], left[0:2], right[0:2], far_right[row : row + 2]], axis=0
            )

        fill(strip_vector, strip_nodes, strip_pre)
        interior(strip_nodes, strip_pre, strip_rate, 2)
        middle = jnp.logical_and(sub >= 2, sub < 6)

        def beside(i, at, edge, lift):
            edge, lift = [jnp.where(first_column, roll(x, 2), x) for x in (edge, lift)]
            edge, lift = [jnp.where(middle, x, 0.0) for x in (edge, lift)]
            parts = (jnp.where(first_column, lift, edge), -lift, jnp.where(first_column, edge, lift))
            for n, x in zip(at, parts):
                strip_rate[i, n] -= x

        outer(nodes, rate, 0, first_column, sub >= 0, across, beside=beside)
        strip_lowest = lax.rem(sub, 2) == 0

        def above(k):
            x = both_sides(k, k)
            return jnp.where(first_column, roll(x, 1), roll(x, -1))

        def strip_upright(line, near, slope):
            at = nodes_of(line, 1)
            u = [[above(27 * i + m) for i in range(5)] for m in at]
            other = [-edge_slope(*x) for x in zip(*u)]
            image = mirrored(near)
            return (
                [jnp.where(strip_lowest, x, y) for x, y in zip(image, u[0])],
                [jnp.where(strip_lowest, x, y) for x, y in zip(slope, other)],
            )

        outer(strip_nodes, strip_rate, 1, strip_lowest, sub >= 0, strip_upright)

        from_left, from_right = sides(WIDE_TILES - 1)

        def in_row(row):
            parts = [from_left[row + 2 : row + 3]] * 2 + [from_left[row : row + 1]]
            parts += [tables[row : row + 1], tables[row + 2 : row + 3]]
            parts += [from_right[row : row + 1]] + [from_right[row + 2 : row + 3]] * 2
            return jnp.concatenate(parts, axis=0)

        code = in_row(0)
        codes[...] = code
        factorize(code, in_row(1), fractions, taken, scaled, factor)
        cut_right(code, rate, strip_rate, scaled, right, ends)


def cut_right(code, rate, strip_rate, scaled, right, ends):
    sub = sublane()
    masks = [code == float(k) for k in (1, 2, 3)]
    odd_sublane = lax.rem(sub, 2) == 1

    def in_row(i, n):
        s, m = strip_rate[i, n], rate[i, n]
        s = jnp.where(odd_sublane, roll(s, 1), s)
        return jnp.where(sub == 3, roll(m, 3), jnp.where(sub == 4, m, s))

    def in_second_row(i, n):
        s, m = strip_rate[i, n], rate[i, n]
        s = jnp.where(sub == 2, roll(s, -1), s)
        return jnp.where(sub == 3, roll(m, 2), jnp.where(sub == 4, roll(m, -1), s))

    left_end = jnp.logical_and(sub == 1, masks[2])
    right_end = jnp.logical_and(sub == 6, masks[0])
    for n in range(NODES):
        c = scaled[n]
        ends[n] = roll(jnp.where(left_end, c, 0.0), -1) + jnp.where(right_end, c, 0.0)
    for c in range(3):
        for i in range(5):
            y = []
            for a in range(3):
                at = [9 * a + 3 * b + c for b in range(3)]
                y.append(below_columns([scaled[n] * in_row(i, n) for n in at]))
            for b in range(3):
                line = [y[a][b] for a in range(3)]
                parts = (above_columns(line), line, below_columns(line))
                for a in range(3):
                    n = 9 * a + 3 * b + c
                    total = weight(a, b, c) * in_second_row(i, n)
                    for k in range(3):
                        total += source_of(jnp.where(masks[k], parts[k][a], 0.0), k)
                    right[i, n] = total


def cut_solve(code, rate, extra, ends, right, factor, done, after):
    sub = sublane()
    is_cut = code > 0.0
    masks = [code == float(k) for k in (1, 2, 3)]
    m_float = masks_of(code)
    has_target = source_of(m_float[0], 0) + m_float[1] + source_of(m_float[2], 2)
    cut = is_cut.astype(jnp.float32)
    cut_low = jnp.logical_and(sub == 0, roll(cut, -3) > 0.0)
    cut_high = jnp.logical_and(sub == 4, is_cut)
    target_low = jnp.logical_and(sub == 1, roll(has_target, -2) > 0.0)
    target_high = jnp.logical_and(sub == 5, roll(has_target, 1) > 0.0)
    for c in range(3):
        x = [[None] * 9 for _ in range(5)]
        for i in range(5):
            y = []
            for a in range(3):
                at = [9 * a + 3 * b + c for b in range(3)]
                y.append(below_columns([ends[n] * extra[i, n] for n in at]))
            for b in range(3):
                line = [y[a][b] for a in range(3)]
                for a, (p, q) in enumerate(zip(below_columns(line), above_columns(line))):
                    p = jnp.where(sub == 0, p, q)
                    x[i][3 * a + b] = right[i, 9 * a + 3 * b + c] + (roll(p, 2) + roll(p, -1))
        for j in range(9):
            for r in range(j + 1, 9):
                f = factor[c, BELOW_DIAGONAL.index((r, j))]
                for i in range(5):
                    x[i][r] = x[i][r] - f * x[i][j]
        for j in range(9):
            f = factor[c, 36 + j]
            for i in range(5):
                x[i][j] = x[i][j] * f
        for r in range(8, 0, -1):
            for j in range(r):
                f = factor[c, BELOW_DIAGONAL.index((r, j))]
                for i in range(5):
                    x[i][j] = x[i][j] - f * x[i][r]
        for i in range(5):
            y = []
            for a in range(3):
                line = [
                    jnp.where(masks[0], roll(s, 1), jnp.where(masks[2], roll(s, -1), s))
                    for s in x[i][3 * a : 3 * a + 3]
                ]
                y.append(below_rows(line))
            for b in range(3):
                line = [y[a][b] for a in range(3)]
                one, three = above_rows(line), below_rows(line)
                for a in range(3):
                    n = 9 * a + 3 * b + c
                    update = jnp.where(masks[0], one[a], jnp.where(masks[2], three[a], line[a]))
                    target = x[i][3 * a + b]
                    m = rate[i, n]
                    m = jnp.where(cut_low, roll(update, -3), jnp.where(cut_high, update, m))
                    m = jnp.where(target_low, roll(target, -2), m)
                    done(i, n, jnp.where(target_high, roll(target, 1), m))
        after(c)


def far_kernel(far, codes, out):
    del codes
    out[...] = far[...]


def last_kernel(
    start,
    nodes,
    rate,
    strip_nodes,
    codes,
    right,
    ends,
    factor,
    wide_a,
    far_a,
    far_b,
    out,
    extra,
    staged,
    sem,
):
    w, n = lax.axis_index("wide"), lax.axis_index("narrow")
    odd, low_pair = lax.rem(w, 2) == 1, lax.rem(w, 4) < 2
    sub = sublane()
    first_column = sub < 4

    copies = [pltpu.make_async_copy(staged.at[:, c], out.at[:, c], sem.at[c]) for c in range(3)]

    def finish(i, n, change):
        k = NODES * i + n
        value = 0.25 * nodes[i, n] + 0.0075 * change
        for k, part in ((k, value[0:4]), (COLUMN + k, value[4:8])):
            staged[k // 3, k % 3] = 0.75 * start[k] + part

    @pl.when(n == 0)
    def _():
        use_far = jnp.logical_xor(first_column, jnp.logical_not(low_pair))

        def value(m):
            tile, row = m // 4, pl.ds(m % 4, 1)
            return jnp.where(use_far, far_a[tile, row, :], far_b[tile, row, :])

        def beyond(line, near, slope):
            at = [9 * i + line for i in range(5)]
            return [value(m) for m in at], [value(45 + m) for m in at]

        outermost = jnp.logical_or(sub == 0, sub == 6)
        outer(strip_nodes, extra, 0, lax.rem(sub, 4) < 2, outermost, beyond, fresh=True)
        cut_solve(codes[...], rate, extra, ends, right, factor, finish, lambda c: copies[c].start())

    def across(line, near, slope):
        def value(a, b):
            return jnp.concatenate([jnp.where(odd, b, a), jnp.where(odd, a, b)], axis=0)

        def both(m):
            return value(far_a[m] if m < FAR_TILES else far_b[m - FAR_TILES], wide_a[m])

        at = [9 * i + line for i in range(5)]
        return [both(m) for m in at], [both(NARROW_TILES + m) for m in at]

    @pl.when(n > 0)
    def _():
        outer(nodes, extra, 0, first_column, sub >= 0, across, fresh=True)
        for c in range(3):
            for k in range(c, COLUMN, 3):
                i, m = divmod(k, NODES)
                finish(i, m, rate[i, m] + extra[i, m])
            copies[c].start()

    for copy in copies:
        copy.wait()


def as_tiles(x):
    return jnp.transpose(x, (0, 2, 3, 1, 4)).reshape(2 * COLUMN, 4, 128)


def from_tiles(x):
    return jnp.transpose(x.reshape(2, 5, NODES, 4, 128), (0, 3, 1, 2, 4))


def device_step(wide, narrow, section_start, section_state, cut_code, cut_rule, rule_fractions):
    f32 = jnp.float32

    def call(kernel, name, shapes, operands, scratch=(), flops=0, out_space=pltpu.VMEM):
        vmem = pl.BlockSpec(memory_space=pltpu.VMEM)
        cost = pl.CostEstimate(flops=flops, bytes_accessed=0, transcendentals=0) if flops else None
        return pl.pallas_call(
            kernel,
            name=name,
            out_shape=[jax.ShapeDtypeStruct(s, f32) for s in shapes],
            in_specs=[vmem] * len(operands),
            out_specs=[pl.BlockSpec(memory_space=out_space)] * len(shapes),
            scratch_shapes=list(scratch),
            cost_estimate=cost,
            compiler_params=pltpu.CompilerParams(vmem_limit_bytes=8 * 2**20),
        )(*operands)

    state, start = as_tiles(section_state), as_tiles(section_start)
    wide_shape, narrow_shape = (WIDE_TILES, 4, 128), (NARROW_TILES, 4, 128)
    (zero,) = call(begin_kernel, "begin", [(8, 128)], (), flops=10**9)
    mine_a, mine_b, tables = call(
        pack_wide,
        "pack_wide",
        [wide_shape, wide_shape, (4, 128)],
        (state, cut_code, cut_rule, zero),
    )
    far_a, far_b = call(
        pack_far, "pack_far", [(FAR_TILES, 4, 128), (SIDE_TILES - FAR_TILES, 4, 128)], (state,)
    )
    (up,) = call(pack_narrow, "pack_narrow", [narrow_shape], (state,))

    both = ("wide", "narrow")
    half = wide // 2
    cross = swaps([(2 * j + 1, (2 * j + 2) % wide) for j in range(half)])
    inside = swaps([(2 * j, 2 * j + 1) for j in range(half)])
    far_inside = swaps([(4 * j + k, 4 * j + 2 + k) for j in range(wide // 4) for k in (0, 1)])
    far_cross = [(4 * j + 2 + k, (4 * j + 4 + k) % wide) for j in range(wide // 4) for k in (0, 1)]
    far_cross = swaps(far_cross)
    even = swaps([(2 * j, 2 * j + 1) for j in range(narrow // 2)])
    between = swaps([(2 * j + 1, 2 * j + 2) for j in range(narrow // 2 - 1)])
    unused = swaps([(16 * j + k, 16 * j + 8 + k) for j in range(wide // 16) for k in range(8)])

    def along_wide(pairs, *rows):
        return [(narrow * a + n, narrow * b + n) for a, b in pairs for n in rows]

    def along_narrow(pairs):
        return [(narrow * w + a, narrow * w + b) for w in range(wide) for a, b in pairs]

    others = range(1, narrow)
    wide_a = lax.ppermute(mine_a, both, along_wide(cross, 0) + along_wide(inside, *others))
    wide_b = lax.ppermute(
        mine_b,
        both,
        along_wide(inside, 0) + along_narrow(between) + along_wide(unused, narrow - 1),
    )
    narrow_got = lax.ppermute(up, both, along_narrow(even))
    far_a = lax.ppermute(far_a, both, along_wide(far_cross, 0) + along_wide(cross, *others))
    far_b = lax.ppermute(far_b, both, along_wide(far_inside, 0) + along_wide(cross, *others))

    full = (5, NODES, 8, 128)
    thermal = pltpu.VMEM((3, NODES, 8, 128), f32)
    nodes, rate = call(inner_kernel, "inner", [full, full], (state,), [thermal], flops=10**9)
    (rate,) = call(wall_kernel, "wall", [full], (nodes, rate, narrow_got), flops=1)
    rate, *strip = call(
        edge_kernel,
        "edge",
        [full, full, (8, 128), full, (NODES, 8, 128), (3, 45, 8, 128)],
        (nodes, rate, wide_a, wide_b, narrow_got, tables, rule_fractions.T, start),
        scratch=[
            pltpu.VMEM((8 * 32, 128), f32),
            thermal,
            pltpu.VMEM(full, f32),
            pltpu.VMEM((NODES, 8, 128), f32),
        ],
        flops=1,
    )
    (far_a,) = call(far_kernel, "far", [far_a.shape], (far_a, strip[1]), flops=10**9)
    (out,) = call(
        last_kernel,
        "last",
        [(2 * COLUMN // 3, 3, 4, 128)],
        (start, nodes, rate, *strip, wide_a, far_a, far_b),
        scratch=[
            pltpu.VMEM(full, f32),
            pltpu.VMEM((2 * COLUMN // 3, 3, 4, 128), f32),
            pltpu.SemaphoreType.DMA((3,)),
        ],
        out_space=pl.ANY,
    )
    return from_tiles(out)


def solution(mesh):
    return jax.shard_map(
        functools.partial(device_step, mesh.shape["wide"], mesh.shape["narrow"]),
        mesh=mesh,
        in_specs=(
            P("wide", "narrow", None, None, None),
            P("wide", "narrow", None, None, None),
            P("wide", None),
            P("wide", None),
            P(),
        ),
        out_specs=P("wide", "narrow", None, None, None),
        check_vma=False,
    )
```

```python
import functools

import jax
import jax.numpy as jnp
from jax import lax
from jax.experimental import pallas as pl
from jax.experimental.pallas import tpu as pltpu
from jax.sharding import PartitionSpec as P

NODES = 27
COLUMN = 5 * NODES
HALF = 68
WIDE_TILES = COLUMN + HALF + 1
NARROW_TILES = 45
FAR_TILES = 24
SIDE_TILES = 2 * NARROW_TILES


def swaps(pairs):
    return [p for a, b in pairs for p in ((a, b), (b, a))]


def nodes_of(line, d):
    base = (line, 9 * (line // 3) + line % 3, 3 * line)[d]
    return [base + (9, 3, 1)[d] * k for k in range(3)]


def sublane():
    return lax.broadcasted_iota(jnp.int32, (8, 128), 0)


def roll(x, shift):
    return pltpu.roll(x, shift % 8, 0)


def edge_slope(near, middle, away):
    return 1.5 * near - 2.0 * middle + 0.5 * away


def edge_of(state, column, i, line, d, high):
    at = [27 * i + k for k in nodes_of(line, d)]
    if column is None:
        u = [jnp.concatenate([state[k], state[COLUMN + k]], axis=0) for k in at]
    else:
        u = [state[column * COLUMN + k] for k in at]
    near, away = jnp.where(high, u[2], u[0]), jnp.where(high, u[0], u[2])
    slope = edge_slope(near, u[1], away)
    return near, jnp.where(high, slope, -slope)


def put_upright(state, target, high):
    for i in range(5):
        for line in range(9):
            near, slope = edge_of(state, None, i, line, 1, high)
            for row, x in ((0, near), (2, slope)):
                target[9 * i + line, row : row + 1, :] = jnp.where(high, x[3:4], x[0:1])
                target[9 * i + line, row + 1 : row + 2, :] = jnp.where(high, x[7:8], x[4:5])


def begin_kernel(zero):
    zero[...] = jnp.zeros_like(zero)


def pack_wide(state, code, rule, zero, wide_a, wide_b, tables):
    del zero
    odd, n = lax.rem(lax.axis_index("wide"), 2), lax.axis_index("narrow")
    for row, table in ((0, code), (1, rule)):
        for column in range(2):
            line = table[column : column + 1, :].astype(jnp.float32)
            tables[2 * column + row : 2 * column + row + 1, :] = line

    @pl.when(n == 0)
    def _():
        for target, near in ((wide_a, odd), (wide_b, 1 - odd)):
            first, other = near * COLUMN, (1 - near) * COLUMN
            target[0:COLUMN] = state[pl.ds(first, COLUMN)]
            for m in range(HALF):
                later = min(m + HALF, COLUMN - 1)
                target[COLUMN + m, 0:2, :] = state[other + m, 0:2, :]
                target[COLUMN + m, 2:4, :] = state[other + later, 0:2, :]
            own, swapped = tables[...], jnp.concatenate([tables[2:4], tables[0:2]], axis=0)
            target[WIDE_TILES - 1] = jnp.where(near == 0, own, swapped)

    @pl.when(n > 0)
    def _():
        put_upright(state, wide_b, lax.rem(n, 2) == 1)
        for i in range(5):
            for line in range(9):
                near, slope = edge_of(state, 1 - odd, i, line, 0, odd == 0)
                wide_a[9 * i + line], wide_a[NARROW_TILES + 9 * i + line] = near, slope


def pack_narrow(state, narrow):
    put_upright(state, narrow, lax.rem(lax.axis_index("narrow"), 2) == 0)


def pack_far(state, far_a, far_b):
    w, n = lax.axis_index("wide"), lax.axis_index("narrow")
    odd, low_pair = lax.rem(w, 2), (lax.rem(w, 4) < 2).astype(jnp.int32)

    @pl.when(n == 0)
    def _():
        for target, column in ((far_a, 1 - low_pair), (far_b, low_pair)):
            for i in range(5):
                for line in range(9):
                    for k, x in zip((0, 45), edge_of(state, column, i, line, 0, column == 1)):
                        m = k + 9 * i + line
                        target[m // 4, m % 4 : m % 4 + 1, :] = x[0:1]

    @pl.when(n > 0)
    def _():
        for i in range(5):
            for line in range(9):
                near, slope = edge_of(state, odd, i, line, 0, odd == 1)
                for m, x in ((9 * i + line, near), (NARROW_TILES + 9 * i + line, slope)):
                    if m < FAR_TILES:
                        far_a[m] = x
                    else:
                        far_b[m - FAR_TILES] = x


def pressure_of(v, inverse):
    return 0.4 * (v[4] - 0.5 * (v[1] * v[1] + v[2] * v[2] + v[3] * v[3]) * inverse)


def flux(v, d, inverse, pressure, sound):
    speed = v[1 + d] * inverse
    out = [v[1 + d], v[1] * speed, v[2] * speed, v[3] * speed, (v[4] + pressure) * speed]
    out[1 + d] = out[1 + d] + pressure
    return out, jnp.abs(speed) + sound


def thermo(v):
    inverse = 1.0 / v[0]
    pressure = pressure_of(v, inverse)
    return inverse, pressure, jnp.sqrt(1.4 * pressure * inverse)


def load(ref, node):
    return [ref[i, node] for i in range(5)]


def fill(vector, nodes, pre):
    for n in range(NODES):
        v = [vector(27 * i + n) for i in range(5)]
        for i in range(5):
            nodes[i, n] = v[i]
        for j, x in enumerate(thermo(v)):
            pre[j, n] = x


def interior(nodes, pre, rate, height):
    sub = sublane()
    inner_x = lax.rem(sub, 2 * height) >= height
    inner_y = lax.rem(sub, height) > 0
    moves = (
        (lambda x: roll(x, height), lambda x: roll(x, -height), inner_x),
        (lambda x: roll(x, 1), lambda x: roll(x, -1), inner_y),
        (lambda x: pltpu.roll(x, 1, 1), lambda x: pltpu.roll(x, 127, 1), None),
    )
    for d in range(3):
        ahead, back, inner = moves[d]

        def body(line, carry, d=d, ahead=ahead, back=back, inner=inner):
            at = nodes_of(line, d)
            v = [load(nodes, n) for n in at]
            f, speeds = zip(*[flux(v[k], d, *[pre[j, at[k]] for j in range(3)]) for k in range(3)])
            speed = 1.5 * jnp.maximum(speeds[0], ahead(speeds[2])) + 0.225
            for i in range(5):
                a, b, c = v[0][i], v[1][i], v[2][i]
                bend = 0.5 * (a + c) - 2.0 * b
                g_low = f[0][i] + 0.1 * (a + bend)
                g_mid = 2.0 * f[1][i] - 0.1 * (c - a)
                g_high = f[2][i] - 0.1 * (c + bend)
                jump = a - ahead(c)
                face = 1.5 * (ahead(g_high) + g_low) - speed * jump
                if inner is not None:
                    face, jump = jnp.where(inner, face, 0.0), jnp.where(inner, jump, 0.0)
                lift = 0.075 * jump
                face_up, lift_up = back(face), back(lift)
                turn = 0.5 * (g_low - g_high)
                above, below = lift_up + turn, lift - turn
                first = face - g_low - g_mid - above
                second = above - lift
                third = below - face_up + g_high + g_mid
                for n, x in zip(at, (first, second, third)):
                    rate[i, n] = x if d == 0 else rate[i, n] + x
            return carry

        for line in range(9):
            body(line, 0)


def outer(nodes, rate, d, lower, active, halo, fresh=False, beside=None, base=None):
    turn = jnp.where(lower, 1.0, -1.0)
    face_sign = 1.5 * turn
    for line in range(9):
        at = nodes_of(line, d)
        v = [load(nodes, n) for n in at]
        near = [jnp.where(lower, a, c) for a, c in zip(v[0], v[2])]
        away = [jnp.where(lower, c, a) for a, c in zip(v[0], v[2])]
        slope = [-turn * edge_slope(*x) for x in zip(near, v[1], away)]
        other, other_slope = halo(line, near, slope)
        f, speed = flux(near, d, *thermo(near))
        f_other, speed_other = flux(other, d, *thermo(other))
        speed = 1.5 * jnp.maximum(speed, speed_other) + 0.225
        for i in range(5):
            gap = near[i] - other[i]
            both = f[i] + f_other[i] - 0.1 * (slope[i] + other_slope[i])
            edge = jnp.where(active, face_sign * both - speed * gap, 0.0)
            lift = jnp.where(active, 0.075 * gap, 0.0)
            parts = (jnp.where(lower, edge, lift), -lift, jnp.where(lower, lift, edge))
            for n, x in zip(at, parts):
                rate[i, n] = x if fresh else (rate if base is None else base)[i, n] + x
            if beside is not None:
                beside(i, at, edge, lift)


def mirrored(v):
    return [v[0], -v[1], -v[2], -v[3], v[4]]


def upright_traces(line, near, slope, pick, wall, top):
    sub = sublane()
    first_column, lowest = sub < 4, lax.rem(sub, 4) == 0
    edge = jnp.logical_or(wall, top)
    other, other_slope = [], []
    image = mirrored(near)
    for i in range(5):
        low, high = pick(9 * i + line)

        def spread(row):
            return jnp.where(
                first_column,
                jnp.where(lowest, low[row : row + 1], high[row : row + 1]),
                jnp.where(lowest, low[row + 1 : row + 2], high[row + 1 : row + 2]),
            )

        other.append(jnp.where(wall, image[i], jnp.where(top, near[i], spread(0))))
        other_slope.append(jnp.where(edge, slope[i], spread(2)))
    return other, other_slope


def wall_kernel(nodes, rate_in, narrow, rate):
    rate[...] = rate_in[...]
    height = lax.rem(sublane(), 4)
    lowest, none = height == 0, height < 0

    def upright(line, near, slope):
        return upright_traces(line, near, slope, lambda m: (narrow[m], narrow[m]), lowest, none)

    @pl.when(lax.axis_index("narrow") == 0)
    def _():
        outer(nodes, rate, 1, lowest, jnp.logical_or(lowest, height == 3), upright)


def inner_kernel(state, nodes, rate, pre):
    fill(lambda k: jnp.concatenate([state[k], state[COLUMN + k]], axis=0), nodes, pre)
    interior(nodes, pre, rate, 4)


def below_rows(x):
    return [6.0 * x[0] - 8.0 * x[1] + 3.0 * x[2], 3.0 * x[0] - 3.0 * x[1] + x[2], x[0]]


def above_rows(x):
    return [x[2], x[0] - 3.0 * x[1] + 3.0 * x[2], 3.0 * x[0] - 8.0 * x[1] + 6.0 * x[2]]


def below_columns(x):
    return [6.0 * x[0] + 3.0 * x[1] + x[2], -8.0 * x[0] - 3.0 * x[1], 3.0 * x[0] + x[1]]


def above_columns(x):
    return [x[1] + 3.0 * x[2], -3.0 * x[1] - 8.0 * x[2], x[0] + 3.0 * x[1] + 6.0 * x[2]]


BELOW = ((6.0, -8.0, 3.0), (3.0, -3.0, 1.0), (1.0, 0.0, 0.0))
ABOVE = ((0.0, 0.0, 1.0), (1.0, -3.0, 3.0), (3.0, -8.0, 6.0))
ENDS = (1.0 / 3.0, 4.0 / 3.0, 1.0 / 3.0)
PAIRS = tuple((i, j) for i in range(3) for j in range(i + 1))
BELOW_DIAGONAL = tuple((r, j) for j in range(9) for r in range(j + 1, 9))


def weight(a, b, c):
    return ENDS[a] * ENDS[b] * ENDS[c]


def combine(table, x, i, j):
    total = None
    for k in range(3):
        factor = table[k][i] * table[k][j]
        if factor != 0.0:
            term = x[k] if factor == 1.0 else factor * x[k]
            total = term if total is None else total + term
    return total


def source_of(x, k):
    return (roll(x, -1), x, roll(x, 1))[k]


def masks_of(code):
    return [(code == float(k)).astype(jnp.float32) for k in (1, 2, 3)]


def factorize(code, rule, fractions, taken, scaled, factor):
    index = lax.broadcasted_iota(jnp.int32, (64, 128), 0).astype(jnp.float32)
    onehot = jnp.concatenate(
        [(index == rule[j : j + 1, :]).astype(jnp.float32) for j in range(8)], axis=1
    )
    shares = lax.dot_general(
        fractions[...],
        onehot,
        (((1,), (0,)), ((), ())),
        precision=lax.Precision.HIGHEST,
        preferred_element_type=jnp.float32,
    )
    for j in range(8):
        taken[32 * j : 32 * j + 27, :] = shares[:, 128 * j : 128 * j + 128]
    is_cut = code > 0.0
    masks = masks_of(code)
    for c in range(3):
        inner = [[None] * 3 for _ in range(3)]
        for a in range(3):
            parts = [[], [], []]
            for b in range(3):
                n = 9 * a + 3 * b + c
                amount = jnp.where(is_cut, weight(a, b, c) * taken[pl.ds(n, 8, stride=32), :], 0.0)
                scaled[n] = amount
                for k in range(3):
                    parts[k].append(source_of(jnp.where(masks[k] > 0.0, amount, 0.0), k))
            for k in range(3):
                inner[k][a] = {p: combine(BELOW, parts[k], *p) for p in PAIRS}
        matrix = {}
        for row in range(9):
            for column in range(row + 1):
                (a, b), (a2, b2) = divmod(row, 3), divmod(column, 3)
                p = (max(b, b2), min(b, b2))
                total = combine(ABOVE, [inner[0][i][p] for i in range(3)], a, a2)
                third = combine(BELOW, [inner[2][i][p] for i in range(3)], a, a2)
                if third is not None:
                    total = third if total is None else total + third
                if a == a2:
                    total = total + inner[1][a][p]
                if row == column:
                    total = total + weight(a, b, c)
                matrix[row, column] = total
        for j in range(9):
            inverse = 1.0 / matrix[j, j]
            factor[c, 36 + j] = inverse
            lower = {r: matrix[r, j] * inverse for r in range(j + 1, 9)}
            for r in range(j + 1, 9):
                factor[c, BELOW_DIAGONAL.index((r, j))] = lower[r]
                for s in range(j + 1, r + 1):
                    matrix[r, s] = matrix[r, s] - lower[r] * matrix[s, j]


def edge_kernel(
    nodes,
    rate_in,
    wide_a,
    wide_b,
    narrow,
    tables,
    fractions,
    start,
    rate,
    strip_nodes,
    codes,
    right,
    ends,
    factor,
    taken,
    strip_pre,
    strip_rate,
    scaled,
):
    del start
    w, n = lax.axis_index("wide"), lax.axis_index("narrow")
    odd = lax.rem(w, 2) == 1
    odd_n, at_bottom, at_top = lax.rem(n, 2) == 1, n == 0, n == lax.axis_size("narrow") - 1
    sub = sublane()
    first_column = sub < 4
    height = lax.rem(sub, 4)

    def sides(k):
        a, b = wide_a[k], wide_b[k]
        return jnp.where(odd, b, a), jnp.where(odd, a, b)

    def both_sides(k_left, k_right):
        return jnp.concatenate([sides(k_left)[0], sides(k_right)[1]], axis=0)

    def across(line, near, slope):
        at = nodes_of(line, 0)
        u = [
            [both_sides(27 * i + at[2 - j], 27 * i + at[j]) for i in range(5)] for j in range(3)
        ]
        other = [edge_slope(*x) for x in zip(*u)]
        return u[0], [jnp.where(first_column, x, -x) for x in other]

    lowest, none = height == 0, height < 0
    top = jnp.logical_and(height == 3, at_top)

    def pick(m):
        a, b = narrow[m], wide_b[m]
        return jnp.where(odd_n, a, b), jnp.where(odd_n, b, a)

    def upright(line, near, slope):
        return upright_traces(line, near, slope, pick, none, top)

    @pl.when(n > 0)
    def _():
        outer(nodes, rate, 1, lowest, jnp.logical_or(lowest, height == 3), upright, base=rate_in)

    @pl.when(at_bottom)
    def _():
        def strip_vector(k):
            left, right = sides(k)
            tile, row = (COLUMN + k, 0) if k < HALF else (COLUMN + k - HALF, 2)
            far_left, far_right = sides(tile)
            return jnp.concatenate(
                [far_left[row : row + 2], left[0:2], right[0:2], far_right[row : row + 2]], axis=0
            )

        fill(strip_vector, strip_nodes, strip_pre)
        interior(strip_nodes, strip_pre, strip_rate, 2)
        middle = jnp.logical_and(sub >= 2, sub < 6)

        def beside(i, at, edge, lift):
            edge, lift = [jnp.where(first_column, roll(x, 2), x) for x in (edge, lift)]
            edge, lift = [jnp.where(middle, x, 0.0) for x in (edge, lift)]
            parts = (jnp.where(first_column, lift, edge), -lift, jnp.where(first_column, edge, lift))
            for n, x in zip(at, parts):
                strip_rate[i, n] -= x

        outer(nodes, rate, 0, first_column, sub >= 0, across, beside=beside, base=rate_in)
        strip_lowest = lax.rem(sub, 2) == 0

        def above(k):
            x = both_sides(k, k)
            return jnp.where(first_column, roll(x, 1), roll(x, -1))

        def strip_upright(line, near, slope):
            at = nodes_of(line, 1)
            u = [[above(27 * i + m) for i in range(5)] for m in at]
            other = [-edge_slope(*x) for x in zip(*u)]
            image = mirrored(near)
            return (
                [jnp.where(strip_lowest, x, y) for x, y in zip(image, u[0])],
                [jnp.where(strip_lowest, x, y) for x, y in zip(slope, other)],
            )

        outer(strip_nodes, strip_rate, 1, strip_lowest, sub >= 0, strip_upright)

        from_left, from_right = sides(WIDE_TILES - 1)

        def in_row(row):
            parts = [from_left[row + 2 : row + 3]] * 2 + [from_left[row : row + 1]]
            parts += [tables[row : row + 1], tables[row + 2 : row + 3]]
            parts += [from_right[row : row + 1]] + [from_right[row + 2 : row + 3]] * 2
            return jnp.concatenate(parts, axis=0)

        code = in_row(0)
        codes[...] = code
        factorize(code, in_row(1), fractions, taken, scaled, factor)
        cut_right(code, rate, strip_rate, scaled, right, ends)


def cut_right(code, rate, strip_rate, scaled, right, ends):
    sub = sublane()
    masks = [code == float(k) for k in (1, 2, 3)]
    odd_sublane = lax.rem(sub, 2) == 1

    def in_row(i, n):
        s, m = strip_rate[i, n], rate[i, n]
        s = jnp.where(odd_sublane, roll(s, 1), s)
        return jnp.where(sub == 3, roll(m, 3), jnp.where(sub == 4, m, s))

    def in_second_row(i, n):
        s, m = strip_rate[i, n], rate[i, n]
        s = jnp.where(sub == 2, roll(s, -1), s)
        return jnp.where(sub == 3, roll(m, 2), jnp.where(sub == 4, roll(m, -1), s))

    left_end = jnp.logical_and(sub == 1, masks[2])
    right_end = jnp.logical_and(sub == 6, masks[0])
    for n in range(NODES):
        c = scaled[n]
        ends[n] = roll(jnp.where(left_end, c, 0.0), -1) + jnp.where(right_end, c, 0.0)
    for c in range(3):
        for i in range(5):
            y = []
            for a in range(3):
                at = [9 * a + 3 * b + c for b in range(3)]
                y.append(below_columns([scaled[n] * in_row(i, n) for n in at]))
            for b in range(3):
                line = [y[a][b] for a in range(3)]
                parts = (above_columns(line), line, below_columns(line))
                for a in range(3):
                    n = 9 * a + 3 * b + c
                    total = weight(a, b, c) * in_second_row(i, n)
                    for k in range(3):
                        total += source_of(jnp.where(masks[k], parts[k][a], 0.0), k)
                    right[i, n] = total


def cut_solve(code, rate, extra, ends, right, factor, done, after):
    sub = sublane()
    is_cut = code > 0.0
    masks = [code == float(k) for k in (1, 2, 3)]
    m_float = masks_of(code)
    has_target = source_of(m_float[0], 0) + m_float[1] + source_of(m_float[2], 2)
    cut = is_cut.astype(jnp.float32)
    cut_low = jnp.logical_and(sub == 0, roll(cut, -3) > 0.0)
    cut_high = jnp.logical_and(sub == 4, is_cut)
    target_low = jnp.logical_and(sub == 1, roll(has_target, -2) > 0.0)
    target_high = jnp.logical_and(sub == 5, roll(has_target, 1) > 0.0)
    for c in range(3):
        x = [[None] * 9 for _ in range(5)]
        for i in range(5):
            y = []
            for a in range(3):
                at = [9 * a + 3 * b + c for b in range(3)]
                y.append(below_columns([ends[n] * extra[i, n] for n in at]))
            for b in range(3):
                line = [y[a][b] for a in range(3)]
                for a, (p, q) in enumerate(zip(below_columns(line), above_columns(line))):
                    p = jnp.where(sub == 0, p, q)
                    x[i][3 * a + b] = right[i, 9 * a + 3 * b + c] + (roll(p, 2) + roll(p, -1))
        for j in range(9):
            for r in range(j + 1, 9):
                f = factor[c, BELOW_DIAGONAL.index((r, j))]
                for i in range(5):
                    x[i][r] = x[i][r] - f * x[i][j]
        for j in range(9):
            f = factor[c, 36 + j]
            for i in range(5):
                x[i][j] = x[i][j] * f
        for r in range(8, 0, -1):
            for j in range(r):
                f = factor[c, BELOW_DIAGONAL.index((r, j))]
                for i in range(5):
                    x[i][j] = x[i][j] - f * x[i][r]
        for i in range(5):
            y = []
            for a in range(3):
                line = [
                    jnp.where(masks[0], roll(s, 1), jnp.where(masks[2], roll(s, -1), s))
                    for s in x[i][3 * a : 3 * a + 3]
                ]
                y.append(below_rows(line))
            for b in range(3):
                line = [y[a][b] for a in range(3)]
                one, three = above_rows(line), below_rows(line)
                for a in range(3):
                    n = 9 * a + 3 * b + c
                    update = jnp.where(masks[0], one[a], jnp.where(masks[2], three[a], line[a]))
                    target = x[i][3 * a + b]
                    m = rate[i, n]
                    m = jnp.where(cut_low, roll(update, -3), jnp.where(cut_high, update, m))
                    m = jnp.where(target_low, roll(target, -2), m)
                    done(i, n, jnp.where(target_high, roll(target, 1), m))
        after(c)


def far_kernel(far, codes, out):
    del codes
    out[...] = far[...]


def last_kernel(
    start,
    nodes,
    rate,
    strip_nodes,
    codes,
    right,
    ends,
    factor,
    wide_a,
    far_a,
    far_b,
    out,
    extra,
    staged,
    sem,
):
    w, n = lax.axis_index("wide"), lax.axis_index("narrow")
    odd, low_pair = lax.rem(w, 2) == 1, lax.rem(w, 4) < 2
    sub = sublane()
    first_column = sub < 4

    copies = [pltpu.make_async_copy(staged.at[:, c], out.at[:, c], sem.at[c]) for c in range(3)]

    def finish(i, n, change):
        k = NODES * i + n
        value = 0.25 * nodes[i, n] + 0.0075 * change
        for k, part in ((k, value[0:4]), (COLUMN + k, value[4:8])):
            staged[k // 3, k % 3] = 0.75 * start[k] + part

    @pl.when(n == 0)
    def _():
        use_far = jnp.logical_xor(first_column, jnp.logical_not(low_pair))

        def value(m):
            tile, row = m // 4, pl.ds(m % 4, 1)
            return jnp.where(use_far, far_a[tile, row, :], far_b[tile, row, :])

        def beyond(line, near, slope):
            at = [9 * i + line for i in range(5)]
            return [value(m) for m in at], [value(45 + m) for m in at]

        outermost = jnp.logical_or(sub == 0, sub == 6)
        outer(strip_nodes, extra, 0, lax.rem(sub, 4) < 2, outermost, beyond, fresh=True)
        cut_solve(codes[...], rate, extra, ends, right, factor, finish, lambda c: copies[c].start())

    def across(line, near, slope):
        def value(a, b):
            return jnp.concatenate([jnp.where(odd, b, a), jnp.where(odd, a, b)], axis=0)

        def both(m):
            return value(far_a[m] if m < FAR_TILES else far_b[m - FAR_TILES], wide_a[m])

        at = [9 * i + line for i in range(5)]
        return [both(m) for m in at], [both(NARROW_TILES + m) for m in at]

    @pl.when(n > 0)
    def _():
        outer(nodes, extra, 0, first_column, sub >= 0, across, fresh=True)
        for c in range(3):
            for k in range(c, COLUMN, 3):
                i, m = divmod(k, NODES)
                finish(i, m, rate[i, m] + extra[i, m])
            copies[c].start()

    for copy in copies:
        copy.wait()


def as_tiles(x):
    return jnp.transpose(x, (0, 2, 3, 1, 4)).reshape(2 * COLUMN, 4, 128)


def from_tiles(x):
    return jnp.transpose(x.reshape(2, 5, NODES, 4, 128), (0, 3, 1, 2, 4))


def device_step(wide, narrow, section_start, section_state, cut_code, cut_rule, rule_fractions):
    f32 = jnp.float32

    def call(kernel, name, shapes, operands, scratch=(), flops=0, out_space=pltpu.VMEM):
        vmem = pl.BlockSpec(memory_space=pltpu.VMEM)
        cost = pl.CostEstimate(flops=flops, bytes_accessed=0, transcendentals=0) if flops else None
        return pl.pallas_call(
            kernel,
            name=name,
            out_shape=[jax.ShapeDtypeStruct(s, f32) for s in shapes],
            in_specs=[vmem] * len(operands),
            out_specs=[pl.BlockSpec(memory_space=out_space)] * len(shapes),
            scratch_shapes=list(scratch),
            cost_estimate=cost,
            compiler_params=pltpu.CompilerParams(vmem_limit_bytes=8 * 2**20),
        )(*operands)

    state, start = as_tiles(section_state), as_tiles(section_start)
    wide_shape, narrow_shape = (WIDE_TILES, 4, 128), (NARROW_TILES, 4, 128)
    (zero,) = call(begin_kernel, "begin", [(8, 128)], (), flops=10**9)
    mine_a, mine_b, tables = call(
        pack_wide,
        "pack_wide",
        [wide_shape, wide_shape, (4, 128)],
        (state, cut_code, cut_rule, zero),
    )
    far_a, far_b = call(
        pack_far, "pack_far", [(FAR_TILES, 4, 128), (SIDE_TILES - FAR_TILES, 4, 128)], (state,)
    )
    (up,) = call(pack_narrow, "pack_narrow", [narrow_shape], (state,))

    both = ("wide", "narrow")
    half = wide // 2
    cross = swaps([(2 * j + 1, (2 * j + 2) % wide) for j in range(half)])
    inside = swaps([(2 * j, 2 * j + 1) for j in range(half)])
    far_inside = swaps([(4 * j + k, 4 * j + 2 + k) for j in range(wide // 4) for k in (0, 1)])
    far_cross = [(4 * j + 2 + k, (4 * j + 4 + k) % wide) for j in range(wide // 4) for k in (0, 1)]
    far_cross = swaps(far_cross)
    even = swaps([(2 * j, 2 * j + 1) for j in range(narrow // 2)])
    between = swaps([(2 * j + 1, 2 * j + 2) for j in range(narrow // 2 - 1)])
    unused = swaps([(16 * j + k, 16 * j + 8 + k) for j in range(wide // 16) for k in range(8)])

    def along_wide(pairs, *rows):
        return [(narrow * a + n, narrow * b + n) for a, b in pairs for n in rows]

    def along_narrow(pairs):
        return [(narrow * w + a, narrow * w + b) for w in range(wide) for a, b in pairs]

    others = range(1, narrow)
    wide_a = lax.ppermute(mine_a, both, along_wide(cross, 0) + along_wide(inside, *others))
    wide_b = lax.ppermute(
        mine_b,
        both,
        along_wide(inside, 0) + along_narrow(between) + along_wide(unused, narrow - 1),
    )
    narrow_got = lax.ppermute(up, both, along_narrow(even))
    far_a = lax.ppermute(far_a, both, along_wide(far_cross, 0) + along_wide(cross, *others))
    far_b = lax.ppermute(far_b, both, along_wide(far_inside, 0) + along_wide(cross, *others))

    full = (5, NODES, 8, 128)
    thermal = pltpu.VMEM((3, NODES, 8, 128), f32)
    nodes, rate = call(inner_kernel, "inner", [full, full], (state,), [thermal], flops=10**9)
    (rate,) = call(wall_kernel, "wall", [full], (nodes, rate, narrow_got), flops=1)
    rate, *strip = call(
        edge_kernel,
        "edge",
        [full, full, (8, 128), full, (NODES, 8, 128), (3, 45, 8, 128)],
        (nodes, rate, wide_a, wide_b, narrow_got, tables, rule_fractions.T, start),
        scratch=[
            pltpu.VMEM((8 * 32, 128), f32),
            thermal,
            pltpu.VMEM(full, f32),
            pltpu.VMEM((NODES, 8, 128), f32),
        ],
        flops=1,
    )
    (far_a,) = call(far_kernel, "far", [far_a.shape], (far_a, strip[1]), flops=10**9)
    (out,) = call(
        last_kernel,
        "last",
        [(2 * COLUMN // 3, 3, 4, 128)],
        (start, nodes, rate, *strip, wide_a, far_a, far_b),
        scratch=[
            pltpu.VMEM(full, f32),
            pltpu.VMEM((2 * COLUMN // 3, 3, 4, 128), f32),
            pltpu.SemaphoreType.DMA((3,)),
        ],
        out_space=pl.ANY,
    )
    return from_tiles(out)


def solution(mesh):
    return jax.shard_map(
        functools.partial(device_step, mesh.shape["wide"], mesh.shape["narrow"]),
        mesh=mesh,
        in_specs=(
            P("wide", "narrow", None, None, None),
            P("wide", "narrow", None, None, None),
            P("wide", None),
            P("wide", None),
            P(),
        ),
        out_specs=P("wide", "narrow", None, None, None),
        check_vma=False,
    )
```
